512 devices in a mesh: gx: 8 (over z_hi, x), gy: 16 (over z_lo, core), gz: 4 (over y).
Axes of the slice: x: 4, y: 4, z: 16 (z_hi: 2, z_lo: 8; z = z_hi * 8 + z_lo), core: 2. Of those that a mesh axis runs over, the one named last changes fastest.
Arguments:
- right_side: float32 [192, 384, 512], P('gx', 'gy', 'gz'), may hold values from -6 to 6
- reaction: float32 [192, 384, 512], P('gx', 'gy', 'gz'), may hold values from 0.05 to 2
- basis_x: float32 [40, 40], replicated, may hold values from -1 to 1
- basis_y: float32 [40, 40], replicated, may hold values from -1 to 1
- basis_z: float32 [144, 144], replicated, may hold values from -0.5 to 0.5
- eigen_x: float32 [40], replicated, may hold values from 0.5 to 6
- eigen_y: float32 [40], replicated, may hold values from 0.5 to 6
- eigen_z: float32 [144], replicated, may hold values from 0.5 to 6
Outputs:
- solution: float32 [192, 384, 512], P('gx', 'gy', 'gz')
The draws below stay inside these ranges and needn't reach their ends.
All inputs are finite; a program needn't handle non-finite values.
Results may differ from the reference program's by a relative error of at most 0.0003.
Values sent between devices are 32-bit elements; how exact they have to be, the bound alone decides.
A program may use at most 64 MiB of HBM per device.

```python
import math
import jax
import jax.numpy as jnp
from jax import lax

CX = 24
CY = 24
CZ = 128
OV = 8
EX = 40
EY = 40
EZ = 144
NX = 192
NY = 384
NZ = 512
N_GX = 8
N_GY = 16
N_GZ = 4


def block_scale(stream_key, shape, pieces, low, high):
    def one(dim, blocks):
        heights = jax.random.uniform(jax.random.fold_in(jax.random.fold_in(stream_key, 6), dim), (blocks,), jnp.float32, low / len(pieces), high / len(pieces))
        return jnp.repeat(jnp.exp(heights), shape[dim] // blocks).reshape((-1,) + (1,) * (len(shape) - dim - 1))

    factor_of = one(*pieces[0])
    for cut in pieces[1:]:
        factor_of = factor_of * one(*cut)
    return factor_of


def normal_values(key, shape, scale, reach, cuts=(), kind=jnp.bfloat16):
    drawn = scale * jax.random.normal(key, shape, jnp.float32)
    if cuts:
        drawn = drawn * block_scale(key, shape, cuts, -0.22, 0.18)
    return jnp.clip(drawn, -reach, reach).astype(kind)


def setup_inputs(seed: int = 0) -> dict:
    keys = jax.random.split(jax.random.key(seed), 9)
    return {
        "right_side": normal_values(keys[0], (NX, NY, NZ), 1.0, 6.0, ((0, 8), (1, 16), (2, 4)), jnp.float32),
        "reaction": jnp.clip(jnp.exp(math.log(2.0) - 3.6888794 * jax.random.uniform(keys[1], (NX, NY, NZ), jnp.float32) ** block_scale(keys[1], (NX, NY, NZ), ((0, 8), (1, 16), (2, 4)), -0.2, 0.2)), 0.05, 2.0),
        "basis_x": normal_values(keys[2], (EX, EX), EX ** -0.5, 1.0, (), jnp.float32),
        "basis_y": normal_values(keys[3], (EY, EY), EY ** -0.5, 1.0, (), jnp.float32),
        "basis_z": normal_values(keys[4], (EZ, EZ), EZ ** -0.5, 0.5, (), jnp.float32),
        "eigen_x": jnp.clip(jnp.exp(jax.random.uniform(keys[5], (EX,), jnp.float32, math.log(0.5), math.log(6.0))), 0.5, 6.0),
        "eigen_y": jnp.clip(jnp.exp(jax.random.uniform(keys[6], (EY,), jnp.float32, math.log(0.5), math.log(6.0))), 0.5, 6.0),
        "eigen_z": jnp.clip(jnp.exp(jax.random.uniform(keys[7], (EZ,), jnp.float32, math.log(0.5), math.log(6.0))), 0.5, 6.0),
    }


def stencil(padded, coefficient):
    center = padded[1:-1, 1:-1, 1:-1]
    sizes = center.shape
    total = coefficient * center
    weights = {1: 0.5, 2: 0.125, 3: 0.0625}
    for offset_x in (-1, 0, 1):
        for offset_y in (-1, 0, 1):
            for offset_z in (-1, 0, 1):
                count = abs(offset_x) + abs(offset_y) + abs(offset_z)
                if count == 0:
                    continue
                neighbour = padded[1 + offset_x:1 + offset_x + sizes[0], 1 + offset_y:1 + offset_y + sizes[1], 1 + offset_z:1 + offset_z + sizes[2]]
                total = total + weights[count] * (center - neighbour)
    return total


def local_solve(block, basis_x, basis_y, basis_z, eigen_x, eigen_y, eigen_z):
    highest = lax.Precision.HIGHEST
    modes = jnp.einsum('ap,abc->pbc', basis_x, block, precision=highest)
    modes = jnp.einsum('bq,pbc->pqc', basis_y, modes, precision=highest)
    modes = jnp.einsum('cs,pqc->pqs', basis_z, modes, precision=highest)
    modes = modes / (eigen_x[:, None, None] + eigen_y[None, :, None] + eigen_z[None, None, :])
    back = jnp.einsum('ap,pqs->aqs', basis_x, modes, precision=highest)
    back = jnp.einsum('bq,aqs->abs', basis_y, back, precision=highest)
    back = jnp.einsum('cs,abs->abc', basis_z, back, precision=highest)
    return back


def reference(right_side, reaction, basis_x, basis_y, basis_z, eigen_x, eigen_y, eigen_z):
    extent = (CX + 2 * OV, CY + 2 * OV, CZ + 2 * OV)

    def schwarz(field):
        padded = jnp.pad(field, OV)
        empty = jnp.zeros(padded.shape, jnp.float32)

        def visit(total, index):
            first_index = index // (N_GY * N_GZ)
            second_index = (index // N_GZ) % N_GY
            third_index = index % N_GZ
            starts = ((first_index * CX).astype(jnp.int32), (second_index * CY).astype(jnp.int32), (third_index * CZ).astype(jnp.int32))
            block = lax.dynamic_slice(padded, starts, extent)
            correction = local_solve(block, basis_x, basis_y, basis_z, eigen_x, eigen_y, eigen_z)
            updated = lax.dynamic_slice(total, starts, extent) + correction
            return lax.dynamic_update_slice(total, updated, starts), None

        total, unused = lax.scan(visit, empty, jnp.arange(N_GX * N_GY * N_GZ, dtype=jnp.int32))
        return total[OV:-OV, OV:-OV, OV:-OV]

    first = schwarz(right_side)
    residual = right_side - stencil(jnp.pad(first, 1), reaction)
    solution = first + schwarz(residual)
    return solution
```

```python
import jax
import jax.numpy as jnp
from jax import lax
from jax.experimental import pallas as pl
from jax.experimental.pallas import tpu as pltpu
from jax.sharding import PartitionSpec as P

MESH = pl.DeviceIdType.MESH
F32 = jnp.float32
BF16 = jnp.bfloat16
DIRS = [(dy, dz) for dy in (-1, 0, 1) for dz in (-1, 0, 1) if (dy, dz) != (0, 0)]
PARTS8 = ((0, 2), (2, 2), (4, 2), (6, 2))
PARTS17 = ((0, 6), (6, 4), (10, 4), (14, 3))


def split(x):
    hi = x.astype(BF16)
    return hi, (x - hi.astype(F32)).astype(BF16)


def mm(a, b):
    return lax.dot_general(a, b, (((1,), (0,)), ((), ())), preferred_element_type=F32)


def roll(x, shift):
    return pltpu.roll(x, shift % x.shape[-1], x.ndim - 1)


def kernel(sizes, f, rea, bx, by, bz, ex, ey, ez, out,
           E0, E1, RE0, RE1, T0, T1, U0, U1, V0, V1, inv, S,
           wz32, wxy32, wzf, wzb, wxf, wxb, wyf, wyb,
           pfA, pfB, pr, pm, pv, pl2H, pl2O,
           rfA, rfB, rr, rmf, rmc, rmy, rvz, rvc, R, RR,
           r2f, r2c, r2y, q2f, q2c, q2y, XL, XR, X2, RB8a, RB17, RB8b,
           ssem, rsem):
    n_gx, n_gy, n_gz = sizes
    gx, gy, gz = (lax.axis_index(a) for a in ("gx", "gy", "gz"))
    relay = n_gx == 8
    mid = n_gx // 2 - 1
    has_y = {-1: gy > 0, 0: gy >= 0, 1: gy < n_gy - 1}
    has_z = {-1: gz > 0, 0: gz >= 0, 1: gz < n_gz - 1}
    has_x = {-1: gx > 0, 1: gx < n_gx - 1}
    has = {d: has_y[d[0]] & has_z[d[1]] for d in DIRS}
    lane = lax.broadcasted_iota(jnp.int32, (8, 128), 1)
    sub = lax.broadcasted_iota(jnp.int32, (8, 128), 0)

    def lanes(rows):
        return lax.broadcasted_iota(jnp.int32, (rows, 128), 1)

    counter = [0]

    def slots(n):
        counter[0] += n
        return counter[0] - n

    def copy(k, src, dst, dev):
        return pltpu.make_async_remote_copy(
            src_ref=src, dst_ref=dst, send_sem=ssem.at[k], recv_sem=rsem.at[k],
            device_id=dev, device_id_type=MESH)

    class YZ:
        def __init__(self, items):
            self.items = {d: items(d) for d in DIRS}
            self.k = {d: slots(len(self.items[d])) for d in DIRS}

        def each(self, d, along):
            dev = (gx, gy + d[0], gz + d[1])
            for j, (src, dst) in enumerate(self.items[along]):
                yield copy(self.k[along] + j, src, dst, dev)

        def start(self):
            for d in DIRS:
                @pl.when(has[d])
                def _():
                    for c in self.each(d, d):
                        c.start()

        def wait(self):
            for d in DIRS:
                @pl.when(has[d])
                def _():
                    for c in self.each(d, (-d[0], -d[1])):
                        c.wait_recv()
                    for c in self.each(d, d):
                        c.wait_send()

    class XX:
        def __init__(self, srcs, dsts, parts=None, rb=None):
            self.srcs, self.dsts, self.rb = srcs, dsts, rb
            self.parts = parts if relay else None
            self.k = {s: slots(1) for s in (-1, 1)}
            if self.parts:
                self.kr = slots(1)
                self.kp = {s: slots(4) for s in (-1, 1)}

        def end(self, s):
            return mid if s == 1 else mid + 1

        def via(self, s, j):
            return self.end(s) - s * j

        def whole(self, s):
            return copy(self.k[s], self.srcs[s], self.dsts[s], (gx + s, gy, gz))

        def part(self, s, j, src=None):
            lo, n = self.parts[j]
            src = self.srcs[s].at[pl.ds(lo, n)] if src is None else src
            return copy(self.kp[s] + j, src, self.dsts[s].at[pl.ds(lo, n)], (self.end(s) + s, gy, gz))

        def leg(self, s, j):
            lo, n = self.parts[j]
            return copy(self.kr, self.srcs[s].at[pl.ds(lo, n)], self.rb.at[pl.ds(0, n)], (self.via(s, j), gy, gz))

        def leg_send(self, s, j):
            lo, n = self.parts[j]
            return pltpu.make_async_remote_copy(
                src_ref=self.srcs[s].at[pl.ds(lo, n)], dst_ref=self.rb.at[pl.ds(0, n)],
                send_sem=ssem.at[self.kp[s] + j], recv_sem=rsem.at[self.kr],
                device_id=(self.via(s, j), gy, gz), device_id_type=MESH)

        def start(self):
            for s in (1, -1):
                if self.parts:
                    @pl.when(has_x[s] & (gx != self.end(s)))
                    def _():
                        self.whole(s).start()

                    @pl.when(gx == self.end(s))
                    def _():
                        for j in (1, 2, 3):
                            self.leg_send(s, j).start()
                        self.part(s, 0).start()
                else:
                    @pl.when(has_x[s])
                    def _():
                        self.whole(s).start()

        def forward(self):
            if self.parts:
                for s in (1, -1):
                    for j in (1, 2, 3):
                        @pl.when(gx == self.via(s, j))
                        def _():
                            self.leg(s, j).wait_recv()
                            self.part(s, j, self.rb.at[pl.ds(0, self.parts[j][1])]).start()

        def wait(self):
            for s in (1, -1):
                if self.parts:
                    @pl.when(has_x[-s] & (gx != self.end(s) + s))
                    def _():
                        self.whole(s).wait_recv()

                    @pl.when(gx == self.end(s) + s)
                    def _():
                        for j in range(4):
                            self.part(s, j).wait_recv()

                    @pl.when(has_x[s] & (gx != self.end(s)))
                    def _():
                        self.whole(s).wait_send()

                    @pl.when(gx == self.end(s))
                    def _():
                        for j in (1, 2, 3):
                            self.leg_send(s, j).wait_send()
                        self.part(s, 0).wait_send()

                    for j in (1, 2, 3):
                        @pl.when(gx == self.via(s, j))
                        def _():
                            self.part(s, j, self.rb.at[pl.ds(0, self.parts[j][1])]).wait_send()
                else:
                    @pl.when(has_x[-s])
                    def _():
                        self.whole(s).wait_recv()

                    @pl.when(has_x[s])
                    def _():
                        self.whole(s).wait_send()

    barrier = pltpu.get_barrier_semaphore()
    expect = jnp.int32(0)
    for d in DIRS:
        @pl.when(has[d])
        def _():
            pl.semaphore_signal(barrier, inc=1, device_id=(gx, gy + d[0], gz + d[1]), device_id_type=MESH)
        expect = expect + has[d].astype(jnp.int32)
    for s in (-1, 1):
        @pl.when(has_x[s])
        def _():
            pl.semaphore_signal(barrier, inc=1, device_id=(gx + s, gy, gz), device_id_type=MESH)
        expect = expect + has_x[s].astype(jnp.int32)
    if relay:
        pairs = []
        for s in (-1, 1):
            e = mid if s == 1 else mid + 1
            pairs += [(e, e - s * j) for j in (2, 3)] + [(e - s * j, e + s) for j in (1, 2, 3)]
        for a, b in pairs:
            for me, other in ((a, b), (b, a)):
                @pl.when(gx == me)
                def _():
                    pl.semaphore_signal(barrier, inc=1, device_id=(jnp.int32(other), gy, gz), device_id_type=MESH)
                expect = expect + (gx == me).astype(jnp.int32)

    def edge(x, width):
        ln = lanes(x.shape[0])
        return jnp.where((ln < width) | (ln >= 128 - width), x, 0.0)

    def pack(dst, load, groups, per, stride, masked):
        def body(g, c):
            acc = None
            for i in range(per):
                x = load(g * per + i)
                if masked:
                    x = edge(x, stride // 2)
                if i:
                    x = roll(x, stride * i)
                acc = x if acc is None else acc + x
            dst[g] = acc
            return c
        lax.fori_loop(0, groups, body, 0)

    def low_part(rows, stride):
        ln = lanes(rows)
        return (lax.rem(ln, stride) < stride // 2) & (ln < 128 - stride // 2 if stride == 18 else ln >= 0)

    def zero_missing(buf_of):
        for d in DIRS:
            bufs = buf_of(d)
            if bufs:
                @pl.when(jnp.logical_not(has[(-d[0], -d[1])]))
                def _():
                    for b in bufs:
                        b[...] = jnp.zeros(b.shape, F32)

    def halo_items(src, x0, nx, dst, packed, recv):
        rows = {0: (0, 24, 0), 1: (16, 8, 32), -1: (0, 8, 24)}

        def items(d):
            s, n, t = rows[d[0]]
            if d[1] == 0:
                return [(src.at[pl.ds(x0 if src is not f and src is not rea else 0, nx), pl.ds(s, n)],
                         dst.at[pl.ds(x0, nx), pl.ds(t, n)])]
            return [(packed.at[:, pl.ds(s, n)], recv.at[0 if d[1] == 1 else 1, :, pl.ds(t, n)])]
        return items

    def fold_items(a0s, packed, recv_f, recv_c, recv_y):
        rows = {1: 24, -1: 32}

        def items(d):
            z = 0 if d[1] == 1 else 1
            y = 0 if d[0] == 1 else 1
            if d[1] == 0:
                return [(U0.at[pl.ds(a, n), pl.ds(rows[d[0]], 8)], recv_y.at[y, pl.ds(t, n)]) for a, n, t in a0s]
            if d[0] == 0:
                return [(packed.at[:, pl.ds(0, 24)], recv_f.at[z])]
            return [(packed.at[:, pl.ds(rows[d[0]], 8)], recv_c.at[y, z])]
        return items

    def layer_items(d):
        z = 0 if d[1] == 1 else 1
        y = 0 if d[0] == 1 else 1
        if d[1] == 0:
            s, t = ((16, 40), (0, 24))[y]
            return [(V0.at[:, pl.ds(s, 8)], V0.at[:, pl.ds(t, 8)]), (R.at[y], RR.at[y])]
        if d[0] == 0:
            return [(pv, rvz.at[z])]
        return [(pv.at[:, pl.ds(8 if y == 0 else 0, 16)], rvc.at[y, z])]

    xf = XX({1: f.at[pl.ds(16, 8)], -1: f.at[pl.ds(0, 8)]},
            {1: E0.at[pl.ds(32, 8), pl.ds(0, 24)], -1: E0.at[pl.ds(24, 8), pl.ds(0, 24)]}, PARTS8, RB8a)
    xr = XX({1: rea.at[pl.ds(16, 8)], -1: rea.at[pl.ds(0, 8)]},
            {1: RE0.at[pl.ds(32, 8), pl.ds(0, 24)], -1: RE0.at[pl.ds(24, 8), pl.ds(0, 24)]})
    fA = YZ(halo_items(f, 0, 24, E0, pfA, rfA))
    fB = YZ(halo_items(E0, 24, 16, E0, pfB, rfB))
    rA = YZ(halo_items(RE0, 0, 40, RE0, pr, rr))
    m1 = YZ(fold_items([(0, 40, 0)], pm, rmf, rmc, rmy))
    m2 = XX({1: S.at[pl.ds(23, 17)], -1: S.at[pl.ds(0, 17)]}, {1: XL, -1: XR}, PARTS17, RB17)
    m3 = YZ(layer_items)
    l2H = YZ(fold_items([(0, 8, 0), (32, 8, 8)], pl2H, r2f, r2c, r2y))
    l2O = YZ(fold_items([(8, 24, 0)], pl2O, q2f, q2c, q2y))
    x2 = XX({1: S.at[pl.ds(32, 8)], -1: S.at[pl.ds(0, 8)]}, {1: X2.at[0], -1: X2.at[1]}, PARTS8, RB8b)

    E0[pl.ds(0, 24), pl.ds(0, 24)] = f[...]
    pack(pfA, lambda i: f[i], 3, 8, 16, True)

    wz32[...] = jnp.zeros((256, 256), F32)
    wz32[0:128, 0:144] = bz[8:136, :]
    wz32[128:136, 0:144] = bz[136:144, :]
    wz32[248:256, 0:144] = bz[0:8, :]
    for w, table in ((wzf, wz32[...]), (wzb, wz32[...].T)):
        hi, lo = split(table)
        w[0:256] = hi
        w[256:512] = hi
        w[512:768] = lo

    def blocks(w, m):
        wxy32[...] = jnp.zeros((80, 256), F32)
        hi, lo = split(m)
        hi, lo = hi.astype(F32), lo.astype(F32)
        for j, part in enumerate((hi, hi, lo)):
            wxy32[0:40, 80 * j:80 * j + 40] = part
            wxy32[40:80, 80 * j + 40:80 * j + 80] = part
        w[...] = wxy32[...].astype(BF16)

    x_nat, y_nat = bx[...], by[...]
    x_circ = jnp.concatenate([x_nat[8:40], x_nat[0:8]], axis=0)
    y_circ = jnp.concatenate([y_nat[8:40], y_nat[0:8]], axis=0)
    blocks(wxf, x_circ.T)
    blocks(wxb, x_nat)
    blocks(wyf, y_circ.T)
    blocks(wyb, y_circ)

    column = lax.broadcasted_iota(jnp.int32, (40, 128), 0)
    exc = lax.fori_loop(0, 40, lambda p, c: jnp.where(column == p, ex[p], c), jnp.zeros((40, 128), F32))
    ez0 = jnp.broadcast_to(ez[:, 0:128], (40, 128))
    ez1 = jnp.broadcast_to(ez[:, 128:256], (40, 128))

    def table(q, c):
        base = exc + ey[q]
        inv[0, q] = 1.0 / (base + ez0)
        inv[1, q] = 1.0 / (base + ez1)
        return c
    lax.fori_loop(0, 40, table, 0)

    def zrows(b, x0, nx, t):
        for i in range(nx // 8):
            b[pl.ds(x0 + 8 * i, 8), pl.ds(t, 8)] = jnp.zeros((8, 8, 128), F32)

    for s, x0 in ((-1, 32), (1, 24)):
        @pl.when(jnp.logical_not(has_x[s]))
        def _():
            for b in (E0, RE0):
                b[pl.ds(x0, 8), pl.ds(0, 24)] = jnp.zeros((8, 24, 128), F32)
            (XL if s == -1 else XR)[...] = jnp.zeros((17, 24, 128), F32)
            X2[0 if s == -1 else 1] = jnp.zeros((8, 24, 128), F32)
    for s, t, tv in ((-1, 32, 40), (1, 24, 24)):
        @pl.when(jnp.logical_not(has_y[s]))
        def _():
            for b in (E0, RE0):
                zrows(b, 0, 40, t)
            zrows(V0, 0, 40, tv)
            V0[pl.ds(40, 2), pl.ds(tv, 8)] = jnp.zeros((2, 8, 128), F32)
            RR[0 if s == -1 else 1] = jnp.zeros((48, 128), F32)
            for b in (rmy, r2y, q2y):
                b[0 if s == -1 else 1] = jnp.zeros(b.shape[1:], F32)

    def missing(d):
        z = 0 if d[1] == 1 else 1
        y = 0 if d[0] == 1 else 1
        t, n = {0: (0, 24), 1: (32, 8), -1: (24, 8)}[d[0]]
        if d[1] == 0:
            return []
        out_ = [b.at[z, :, pl.ds(t, n)] for b in (rfA, rfB, rr)]
        if d[0] == 0:
            return out_ + [b.at[z] for b in (rmf, r2f, q2f, rvz)]
        return out_ + [b.at[y, z] for b in (rmc, r2c, q2c, rvc)]
    zero_missing(missing)

    pl.semaphore_wait(barrier, expect)

    def unpack_halo(recv, g0, groups, dst1, x0):
        def body(g, c):
            both = jnp.where(low_part(40, 16), recv[1, g], recv[0, g])
            for i in range(8):
                dst1[x0 + g * 8 + i] = edge(roll(both, -16 * i), 8)
            return c
        lax.fori_loop(g0, g0 + groups, body, 0)

    def cat3(x0, x1):
        h0, l0 = split(x0)
        h1, l1 = split(x1)
        return jnp.concatenate([h0, h1, l0, l1, h0, h1], axis=1)

    def stack3(x):
        hi, lo = split(x)
        return jnp.concatenate([hi, lo, hi], axis=0)

    def forward_chunk(c, _):
        x0 = E0[pl.ds(8 * c, 8)].reshape(320, 128)
        x1 = E1[pl.ds(8 * c, 8)].reshape(320, 128)
        z = mm(cat3(x0, x1), wzf[...])
        for i in range(4):
            y = mm(wyf[:, 0:240], stack3(z[80 * i:80 * i + 80]))
            T0[pl.ds(320 * c + 80 * i, 80), :] = y[:, 0:128]
            T1[pl.ds(320 * c + 80 * i, 80), :] = y[:, 128:256]
        return _

    def middle(j, _):
        parts = []
        for i in range(2):
            q = 2 * j + i
            parts.append(jnp.concatenate([T0[pl.ds(q, 40, stride=40), :], T1[pl.ds(q, 40, stride=40), :]], axis=1))
        m = mm(wxf[:, 0:240], stack3(jnp.concatenate(parts, axis=0)))
        scale = jnp.concatenate([
            jnp.concatenate([inv[0, 2 * j + i], inv[1, 2 * j + i]], axis=1) for i in range(2)], axis=0)
        m = mm(wxb[:, 0:240], stack3(m * scale))
        for i in range(2):
            q = 2 * j + i
            T0[pl.ds(q, 40, stride=40), :] = m[40 * i:40 * i + 40, 0:128]
            T1[pl.ds(q, 40, stride=40), :] = m[40 * i:40 * i + 40, 128:256]
        return _

    def back_chunk(c, _):
        parts = []
        for i in range(4):
            x = jnp.concatenate([T0[pl.ds(320 * c + 80 * i, 80), :], T1[pl.ds(320 * c + 80 * i, 80), :]], axis=1)
            parts.append(mm(wyb[:, 0:240], stack3(x)))
        y = jnp.concatenate(parts, axis=0)
        z = mm(cat3(y[:, 0:128], y[:, 128:256]), wzb[...])
        U0[pl.ds(8 * c, 8)] = z[:, 0:128].reshape(8, 40, 128)
        U1[pl.ds(8 * c, 8)] = z[:, 128:256].reshape(8, 40, 128)
        return _

    def fold(a0, g0, groups, y0, recv_f, recv_c, recv_y):
        def body(g, c):
            both = jnp.where(low_part(24, 16), recv_f[0, g], recv_f[1, g])
            low = low_part(8, 16)
            first = jnp.where(low, recv_c[0, 0, g], recv_c[0, 1, g])
            last = jnp.where(low, recv_c[1, 0, g], recv_c[1, 1, g])
            both = both + jnp.concatenate([first, jnp.zeros((8, 128), F32), last], axis=0)
            for i in range(8):
                a = a0 + 8 * (g - g0) + i
                t = y0 + 8 * (g - g0) + i
                zpart = edge(roll(both, -16 * i), 8)
                ypart = jnp.concatenate([recv_y[0, t], jnp.zeros((8, 128), F32), recv_y[1, t]], axis=0)
                S[a] = U0[a, pl.ds(0, 24)] + (zpart + ypart)
            return c
        lax.fori_loop(g0, g0 + groups, body, 0)

    xf.start()
    fA.start()
    xf.forward()
    fA.wait()
    unpack_halo(rfA, 0, 3, E1, 0)
    lax.fori_loop(0, 3, forward_chunk, 0)
    xf.wait()
    pack(pfB, lambda i: E0[24 + i, pl.ds(0, 24)], 2, 8, 16, True)
    fB.start()
    xr.start()
    fB.wait()
    unpack_halo(rfB, 0, 2, E1, 24)
    lax.fori_loop(3, 5, forward_chunk, 0)
    lax.fori_loop(0, 20, middle, 0)
    lax.fori_loop(0, 5, back_chunk, 0)
    pack(pm, lambda i: U1[i], 5, 8, 16, False)
    m1.start()
    m1.wait()
    fold(0, 0, 5, 0, rmf, rmc, rmy)
    m2.start()
    m2.forward()

    RE0[pl.ds(0, 24), pl.ds(0, 24)] = rea[...]
    xr.wait()
    pack(pr, lambda i: RE0[i, pl.ds(0, 24)], 5, 8, 16, True)
    rA.start()
    rA.wait()
    unpack_halo(rr, 0, 5, RE1, 0)
    m2.wait()

    def build_a(i, c):
        V0[i + 1, pl.ds(0, 24)] = S[i] + XL[i + 1]
        V0[i + 25, pl.ds(0, 24)] = S[i + 24] + XR[i]
        return c
    lax.fori_loop(0, 16, build_a, 0)
    for i in range(8):
        V0[17 + i, pl.ds(0, 24)] = S[16 + i]
    V0[0, pl.ds(0, 24)] = XL[0]
    V0[41, pl.ds(0, 24)] = XR[16]
    for s, v in ((-1, 0), (1, 33)):
        @pl.when(jnp.logical_not(has_x[s]))
        def _():
            V0[pl.ds(v, 9), pl.ds(0, 24)] = jnp.zeros((9, 24, 128), F32)
    R[...] = jnp.zeros((2, 48, 128), F32)
    for i in range(42):
        R[0, i:i + 1, :] = V0[i, 15:16, :]
        R[1, i:i + 1, :] = V0[i, 8:9, :]
    pack(pv, lambda i: V0[i, pl.ds(0, 24)], 6, 7, 18, True)
    m3.start()
    m3.wait()
    for i in range(42):
        V0[i, 39:40, :] = RR[0, i:i + 1, :]
        V0[i, 32:33, :] = RR[1, i:i + 1, :]

    def unpack_layer(g, c):
        face = jnp.where(low_part(24, 18), rvz[1, g], rvz[0, g])
        low = low_part(16, 18)
        lo_y = jnp.where(low, rvc[0, 1, g], rvc[0, 0, g])
        hi_y = jnp.where(low, rvc[1, 1, g], rvc[1, 0, g])
        between = jnp.where(sub == 0, hi_y[8:16], lo_y[0:8])
        both = jnp.concatenate([face, hi_y[0:8], between, lo_y[8:16]], axis=0)
        for i in range(7):
            V1[g * 7 + i] = edge(roll(both, -18 * i), 9)
        return c
    lax.fori_loop(0, 6, unpack_layer, 0)

    row = lax.broadcasted_iota(jnp.int32, (40, 128), 0)
    ln = lanes(40)
    inside_y = jnp.logical_not(((row >= 24) & (row < 32) & jnp.logical_not(has_y[1]))
                               | ((row >= 32) & jnp.logical_not(has_y[-1])))
    mask0 = jnp.where(inside_y, 1.0, 0.0)
    mask1 = jnp.where(inside_y & (((ln < 8) & has_z[1]) | ((ln >= 120) & has_z[-1])), 1.0, 0.0)
    ln48 = lanes(48)

    def shifts(v0, v1):
        p0, p1 = roll(v0, -1), roll(v1, -1)
        n0, n1 = roll(v0, 1), roll(v1, 1)
        top, bottom = ln48 == 127, ln48 == 0
        z0 = jnp.where(top, p1, p0) + jnp.where(bottom, n1, n0)
        z1 = jnp.where(top, p0, p1) + jnp.where(bottom, n0, n1)
        return z0 + 2.0 * v0, z1 + 2.0 * v1

    def sum_y(x):
        return pltpu.roll(x, 47, 0) + pltpu.roll(x, 1, 0)

    def level(v):
        v0, v1 = V0[v], V1[v]
        a0, a1 = shifts(v0, v1)
        b0, b1 = sum_y(a0) + 2.0 * a0, sum_y(a1) + 2.0 * a1
        return a0, a1, b0, b1

    def ext(x):
        return jnp.concatenate([x[0:32], x[40:48]], axis=0)

    def stencil(a, c):
        bm0, bm1, a0, a1, b0, b1 = c
        na0, na1, nb0, nb1 = level(a + 2)
        x = jnp.where(a < 8, a + 32, a - 8)
        inside = jnp.where(((a < 8) & jnp.logical_not(has_x[-1])) | ((a >= 32) & jnp.logical_not(has_x[1])), 0.0, 1.0)
        for V, E, RE, m, bm, aa, b, nb in ((V0, E0, RE0, mask0, bm0, a0, b0, nb0), (V1, E1, RE1, mask1, bm1, a1, b1, nb1)):
            v = V[a + 1]
            axis = V[a] + V[a + 2] + sum_y(v) + (aa - 2.0 * v)
            k = 5.5 * v - 0.25 * axis - 0.0625 * (bm + nb + 2.0 * b)
            E[x] = (E[x] - (RE[x] * ext(v) + ext(k))) * (m * inside)
        return b0, b1, na0, na1, nb0, nb1

    l0 = level(0)
    l1 = level(1)
    lax.fori_loop(0, 40, stencil, (l0[2], l0[3], l1[0], l1[1], l1[2], l1[3]))

    lax.fori_loop(0, 5, forward_chunk, 0)
    lax.fori_loop(0, 20, middle, 0)
    back_chunk(0, 0)
    back_chunk(4, 0)
    pack(pl2H, lambda i: U1[jnp.where(i < 8, i, i + 24)], 2, 8, 16, False)
    l2H.start()
    lax.fori_loop(1, 4, back_chunk, 0)
    pack(pl2O, lambda i: U1[i + 8], 3, 8, 16, False)
    l2O.start()
    l2H.wait()
    fold(0, 0, 1, 0, r2f, r2c, r2y)
    fold(32, 1, 1, 8, r2f, r2c, r2y)
    x2.start()
    x2.forward()
    l2O.wait()
    fold(8, 0, 3, 0, q2f, q2c, q2y)
    x2.wait()

    def finish(i, c):
        out[i] = V0[i + 9, pl.ds(0, 24)] + (S[i + 8] + X2[0, i])
        out[i + 8] = V0[i + 17, pl.ds(0, 24)] + S[i + 16]
        out[i + 16] = V0[i + 25, pl.ds(0, 24)] + (S[i + 24] + X2[1, i])
        return c
    lax.fori_loop(0, 8, finish, 0)


def solution(mesh):
    sizes = tuple(mesh.shape[a] for a in ("gx", "gy", "gz"))

    def local(right_side, reaction, basis_x, basis_y, basis_z, eigen_x, eigen_y, eigen_z):
        def vm(*shape, dtype=F32):
            return pltpu.VMEM(shape, dtype)
        scratch = [vm(40, 40, 128), vm(40, 40, 128), vm(40, 40, 128), vm(40, 40, 128),
                   vm(1600, 128), vm(1600, 128), vm(40, 40, 128), vm(40, 40, 128),
                   vm(42, 48, 128), vm(42, 48, 128), vm(2, 40, 40, 128), vm(40, 24, 128),
                   vm(256, 256), vm(80, 256), vm(768, 256, dtype=BF16), vm(768, 256, dtype=BF16)]
        scratch += [vm(80, 256, dtype=BF16)] * 4
        scratch += [vm(3, 24, 128), vm(2, 24, 128), vm(5, 24, 128), vm(5, 40, 128), vm(6, 24, 128),
                    vm(2, 40, 128), vm(3, 40, 128)]
        scratch += [vm(2, 3, 40, 128), vm(2, 2, 40, 128), vm(2, 5, 40, 128),
                    vm(2, 5, 24, 128), vm(2, 2, 5, 8, 128), vm(2, 40, 8, 128),
                    vm(2, 6, 24, 128), vm(2, 2, 6, 16, 128), vm(2, 48, 128), vm(2, 48, 128),
                    vm(2, 2, 24, 128), vm(2, 2, 2, 8, 128), vm(2, 16, 8, 128),
                    vm(2, 3, 24, 128), vm(2, 2, 3, 8, 128), vm(2, 24, 8, 128),
                    vm(17, 24, 128), vm(17, 24, 128), vm(2, 8, 24, 128),
                    vm(2, 24, 128), vm(4, 24, 128), vm(2, 24, 128),
                    pltpu.SemaphoreType.DMA((120,)), pltpu.SemaphoreType.DMA((120,))]
        vmem = pl.BlockSpec(memory_space=pltpu.VMEM)
        smem = pl.BlockSpec(memory_space=pltpu.SMEM)
        row_z = jnp.pad(eigen_z, (0, 112), constant_values=1.0).reshape(1, 256)

        def body(*refs):
            kernel(sizes, *refs)

        return pl.pallas_call(
            body,
            out_shape=jax.ShapeDtypeStruct((24, 24, 128), F32),
            in_specs=[vmem] * 5 + [smem, smem, vmem],
            out_specs=vmem,
            scratch_shapes=scratch,
            compiler_params=pltpu.CompilerParams(
                collective_id=0, has_side_effects=True, vmem_limit_bytes=40 * 1024 * 1024),
            cost_estimate=pl.CostEstimate(flops=1200000000, bytes_accessed=2000000, transcendentals=0),
        )(right_side, reaction, basis_x, basis_y, basis_z, eigen_x, eigen_y, row_z)

    return jax.shard_map(
        local,
        mesh=mesh,
        in_specs=(P("gx", "gy", "gz"), P("gx", "gy", "gz"), P(), P(), P(), P(), P(), P()),
        out_specs=P("gx", "gy", "gz"),
        check_vma=False,
    )
```

```python
import jax
import jax.numpy as jnp
from jax import lax
from jax.experimental import pallas as pl
from jax.experimental.pallas import tpu as pltpu
from jax.sharding import PartitionSpec as P

MESH = pl.DeviceIdType.MESH
F32 = jnp.float32
BF16 = jnp.bfloat16
UL, US, UM, UF, UB = 3, 4, 10, True, True
DIRS = [(dy, dz) for dy in (-1, 0, 1) for dz in (-1, 0, 1) if (dy, dz) != (0, 0)]
PARTS8 = ((0, 2), (2, 2), (4, 2), (6, 2))
PARTS17 = ((0, 6), (6, 4), (10, 4), (14, 3))


def split(x):
    hi = x.astype(BF16)
    return hi, (x - hi.astype(F32)).astype(BF16)


def mm(a, b):
    return lax.dot_general(a, b, (((1,), (0,)), ((), ())), preferred_element_type=F32)


def roll(x, shift):
    return pltpu.roll(x, shift % x.shape[-1], x.ndim - 1)


def kernel(sizes, f_hbm, rea_hbm, bx_hbm, by_hbm, bz_hbm, ex, ey, ez, out,
           f, rea, bx, by, bz,
           E0, E1, RE0, RE1, T0, T1, U0, U1, V0, V1, inv, S,
           A0, A1, wz32, wxy32, wzf, wzb, wxf, wxb, wyf, wyb,
           pfA, pfB, pr, pm, pv, pl2H, pl2O,
           rfA, rfB, rr, rmf, rmc, rmy, rvz, rvc, R, RR,
           r2f, r2c, r2y, q2f, q2c, q2y, XL, XR, X2, RB8a, RB17, RB8b,
           ssem, rsem, lsem):
    n_gx, n_gy, n_gz = sizes
    gx, gy, gz = (lax.axis_index(a) for a in ("gx", "gy", "gz"))
    relay = n_gx == 8
    mid = n_gx // 2 - 1
    has_y = {-1: gy > 0, 0: gy >= 0, 1: gy < n_gy - 1}
    has_z = {-1: gz > 0, 0: gz >= 0, 1: gz < n_gz - 1}
    has_x = {-1: gx > 0, 1: gx < n_gx - 1}
    has = {d: has_y[d[0]] & has_z[d[1]] for d in DIRS}
    lane = lax.broadcasted_iota(jnp.int32, (8, 128), 1)
    sub = lax.broadcasted_iota(jnp.int32, (8, 128), 0)

    def lanes(rows):
        return lax.broadcasted_iota(jnp.int32, (rows, 128), 1)

    counter = [0]

    def slots(n):
        counter[0] += n
        return counter[0] - n

    def copy(k, src, dst, dev):
        return pltpu.make_async_remote_copy(
            src_ref=src, dst_ref=dst, send_sem=ssem.at[k], recv_sem=rsem.at[k],
            device_id=dev, device_id_type=MESH)

    class YZ:
        def __init__(self, items):
            self.items = {d: items(d) for d in DIRS}
            self.k = {d: slots(len(self.items[d])) for d in DIRS}

        def each(self, d, along):
            dev = (gx, gy + d[0], gz + d[1])
            for j, (src, dst) in enumerate(self.items[along]):
                yield copy(self.k[along] + j, src, dst, dev)

        def start(self):
            for d in DIRS:
                @pl.when(has[d])
                def _():
                    for c in self.each(d, d):
                        c.start()

        def wait(self):
            for d in DIRS:
                @pl.when(has[d])
                def _():
                    for c in self.each(d, (-d[0], -d[1])):
                        c.wait_recv()
                    for c in self.each(d, d):
                        c.wait_send()

    class XX:
        def __init__(self, srcs, dsts, parts=None, rb=None):
            self.srcs, self.dsts, self.rb = srcs, dsts, rb
            self.parts = parts if relay else None
            self.k = {s: slots(1) for s in (-1, 1)}
            if self.parts:
                self.kr = slots(1)
                self.kp = {s: slots(4) for s in (-1, 1)}

        def end(self, s):
            return mid if s == 1 else mid + 1

        def via(self, s, j):
            return self.end(s) - s * j

        def whole(self, s):
            return copy(self.k[s], self.srcs[s], self.dsts[s], (gx + s, gy, gz))

        def part(self, s, j, src=None):
            lo, n = self.parts[j]
            src = self.srcs[s].at[pl.ds(lo, n)] if src is None else src
            return copy(self.kp[s] + j, src, self.dsts[s].at[pl.ds(lo, n)], (self.end(s) + s, gy, gz))

        def leg(self, s, j):
            lo, n = self.parts[j]
            return copy(self.kr, self.srcs[s].at[pl.ds(lo, n)], self.rb.at[pl.ds(0, n)], (self.via(s, j), gy, gz))

        def leg_send(self, s, j):
            lo, n = self.parts[j]
            return pltpu.make_async_remote_copy(
                src_ref=self.srcs[s].at[pl.ds(lo, n)], dst_ref=self.rb.at[pl.ds(0, n)],
                send_sem=ssem.at[self.kp[s] + j], recv_sem=rsem.at[self.kr],
                device_id=(self.via(s, j), gy, gz), device_id_type=MESH)

        def start(self):
            for s in (1, -1):
                if self.parts:
                    @pl.when(has_x[s] & (gx != self.end(s)))
                    def _():
                        self.whole(s).start()

                    @pl.when(gx == self.end(s))
                    def _():
                        for j in (1, 2, 3):
                            self.leg_send(s, j).start()
                        self.part(s, 0).start()
                else:
                    @pl.when(has_x[s])
                    def _():
                        self.whole(s).start()

        def forward(self):
            if self.parts:
                for s in (1, -1):
                    for j in (1, 2, 3):
                        @pl.when(gx == self.via(s, j))
                        def _():
                            self.leg(s, j).wait_recv()
                            self.part(s, j, self.rb.at[pl.ds(0, self.parts[j][1])]).start()

        def wait(self):
            for s in (1, -1):
                if self.parts:
                    @pl.when(has_x[-s] & (gx != self.end(s) + s))
                    def _():
                        self.whole(s).wait_recv()

                    @pl.when(gx == self.end(s) + s)
                    def _():
                        for j in range(4):
                            self.part(s, j).wait_recv()

                    @pl.when(has_x[s] & (gx != self.end(s)))
                    def _():
                        self.whole(s).wait_send()

                    @pl.when(gx == self.end(s))
                    def _():
                        for j in (1, 2, 3):
                            self.leg_send(s, j).wait_send()
                        self.part(s, 0).wait_send()

                    for j in (1, 2, 3):
                        @pl.when(gx == self.via(s, j))
                        def _():
                            self.part(s, j, self.rb.at[pl.ds(0, self.parts[j][1])]).wait_send()
                else:
                    @pl.when(has_x[-s])
                    def _():
                        self.whole(s).wait_recv()

                    @pl.when(has_x[s])
                    def _():
                        self.whole(s).wait_send()

    barrier = pltpu.get_barrier_semaphore()
    expect = jnp.int32(0)
    for d in DIRS:
        @pl.when(has[d])
        def _():
            pl.semaphore_signal(barrier, inc=1, device_id=(gx, gy + d[0], gz + d[1]), device_id_type=MESH)
        expect = expect + has[d].astype(jnp.int32)
    for s in (-1, 1):
        @pl.when(has_x[s])
        def _():
            pl.semaphore_signal(barrier, inc=1, device_id=(gx + s, gy, gz), device_id_type=MESH)
        expect = expect + has_x[s].astype(jnp.int32)
    if relay:
        pairs = []
        for s in (-1, 1):
            e = mid if s == 1 else mid + 1
            pairs += [(e, e - s * j) for j in (2, 3)] + [(e - s * j, e + s) for j in (1, 2, 3)]
        for a, b in pairs:
            for me, other in ((a, b), (b, a)):
                @pl.when(gx == me)
                def _():
                    pl.semaphore_signal(barrier, inc=1, device_id=(jnp.int32(other), gy, gz), device_id_type=MESH)
                expect = expect + (gx == me).astype(jnp.int32)

    loads = [pltpu.make_async_copy(a, b, lsem.at[i]) for i, (a, b) in enumerate(
        ((f_hbm, f), (bz_hbm, bz), (bx_hbm, bx), (by_hbm, by), (rea_hbm, rea)))]
    for c in loads:
        c.start()
    for c in loads[:4]:
        c.wait()

    def edge(x, width):
        ln = lanes(x.shape[0])
        return jnp.where((ln < width) | (ln >= 128 - width), x, 0.0)

    def pack(dst, load, groups, per, stride, masked):
        def body(g, c):
            acc = None
            for i in range(per):
                x = load(g * per + i)
                if masked:
                    x = edge(x, stride // 2)
                if i:
                    x = roll(x, stride * i)
                acc = x if acc is None else acc + x
            dst[g] = acc
            return c
        lax.fori_loop(0, groups, body, 0)

    def low_part(rows, stride):
        ln = lanes(rows)
        return (lax.rem(ln, stride) < stride // 2) & (ln < 128 - stride // 2 if stride == 18 else ln >= 0)

    def zero_missing(buf_of):
        for d in DIRS:
            bufs = buf_of(d)
            if bufs:
                @pl.when(jnp.logical_not(has[(-d[0], -d[1])]))
                def _():
                    for b in bufs:
                        b[...] = jnp.zeros(b.shape, F32)

    def halo_items(src, x0, nx, dst, packed, recv):
        rows = {0: (0, 24, 0), 1: (16, 8, 32), -1: (0, 8, 24)}

        def items(d):
            s, n, t = rows[d[0]]
            if d[1] == 0:
                return [(src.at[pl.ds(x0 if src is not f and src is not rea else 0, nx), pl.ds(s, n)],
                         dst.at[pl.ds(x0, nx), pl.ds(t, n)])]
            return [(packed.at[:, pl.ds(s, n)], recv.at[0 if d[1] == 1 else 1, :, pl.ds(t, n)])]
        return items

    def fold_items(a0s, packed, recv_f, recv_c, recv_y):
        rows = {1: 24, -1: 32}

        def items(d):
            z = 0 if d[1] == 1 else 1
            y = 0 if d[0] == 1 else 1
            if d[1] == 0:
                return [(U0.at[pl.ds(a, n), pl.ds(rows[d[0]], 8)], recv_y.at[y, pl.ds(t, n)]) for a, n, t in a0s]
            if d[0] == 0:
                return [(packed.at[:, pl.ds(0, 24)], recv_f.at[z])]
            return [(packed.at[:, pl.ds(rows[d[0]], 8)], recv_c.at[y, z])]
        return items

    def layer_items(d):
        z = 0 if d[1] == 1 else 1
        y = 0 if d[0] == 1 else 1
        if d[1] == 0:
            s, t = ((16, 40), (0, 24))[y]
            return [(V0.at[:, pl.ds(s, 8)], V0.at[:, pl.ds(t, 8)]), (R.at[y], RR.at[y])]
        if d[0] == 0:
            return [(pv, rvz.at[z])]
        return [(pv.at[:, pl.ds(8 if y == 0 else 0, 16)], rvc.at[y, z])]

    xf = XX({1: f.at[pl.ds(16, 8)], -1: f.at[pl.ds(0, 8)]},
            {1: E0.at[pl.ds(32, 8), pl.ds(0, 24)], -1: E0.at[pl.ds(24, 8), pl.ds(0, 24)]}, PARTS8, RB8a)
    xr = XX({1: rea.at[pl.ds(16, 8)], -1: rea.at[pl.ds(0, 8)]},
            {1: RE0.at[pl.ds(32, 8), pl.ds(0, 24)], -1: RE0.at[pl.ds(24, 8), pl.ds(0, 24)]})
    fA = YZ(halo_items(f, 0, 24, E0, pfA, rfA))
    fB = YZ(halo_items(E0, 24, 16, E0, pfB, rfB))
    rA = YZ(halo_items(RE0, 0, 40, RE0, pr, rr))
    m1 = YZ(fold_items([(0, 40, 0)], pm, rmf, rmc, rmy))
    m2 = XX({1: S.at[pl.ds(23, 17)], -1: S.at[pl.ds(0, 17)]}, {1: XL, -1: XR}, PARTS17, RB17)
    m3 = YZ(layer_items)
    l2H = YZ(fold_items([(0, 8, 0), (32, 8, 8)], pl2H, r2f, r2c, r2y))
    l2O = YZ(fold_items([(8, 24, 0)], pl2O, q2f, q2c, q2y))
    x2 = XX({1: S.at[pl.ds(32, 8)], -1: S.at[pl.ds(0, 8)]}, {1: X2.at[0], -1: X2.at[1]}, PARTS8, RB8b)

    E0[pl.ds(0, 24), pl.ds(0, 24)] = f[...]
    pack(pfA, lambda i: f[i], 3, 8, 16, True)

    wz32[...] = jnp.zeros((256, 256), F32)
    wz32[0:128, 0:144] = bz[8:136, :]
    wz32[128:136, 0:144] = bz[136:144, :]
    wz32[248:256, 0:144] = bz[0:8, :]
    for w, table, turned in ((wzf, wz32[...], True), (wzb, wz32[...].T, False)):
        hi, lo = split(table)
        w[0:128] = hi[0:128]
        w[128:256] = hi[0:128]
        w[256:384] = lo[0:128]
        hi, lo = hi.astype(F32)[128:256], lo.astype(F32)[128:256]
        if turned:
            tail = jnp.concatenate([hi[0:8], hi[120:128], hi[0:8], lo[120:128], lo[0:8],
                                    jnp.zeros((80, 256), F32), hi[120:128]], axis=0)
        else:
            tail = jnp.concatenate([hi[0:16], hi[0:16], lo[0:16], jnp.zeros((80, 256), F32)], axis=0)
        w[384:512] = tail.astype(BF16)

    def blocks(w, m):
        wxy32[...] = jnp.zeros((80, 256), F32)
        hi, lo = split(m)
        hi, lo = hi.astype(F32), lo.astype(F32)
        for j, part in enumerate((hi, hi, lo)):
            wxy32[0:40, 80 * j:80 * j + 40] = part
            wxy32[40:80, 80 * j + 40:80 * j + 80] = part
        w[...] = wxy32[...].astype(BF16)

    x_nat, y_nat = bx[...], by[...]
    x_circ = jnp.concatenate([x_nat[8:40], x_nat[0:8]], axis=0)
    y_circ = jnp.concatenate([y_nat[8:40], y_nat[0:8]], axis=0)
    blocks(wxf, x_circ.T)
    blocks(wxb, x_nat)
    blocks(wyf, y_circ.T)
    blocks(wyb, y_circ)

    column = lax.broadcasted_iota(jnp.int32, (40, 128), 0)
    exc = lax.fori_loop(0, 40, lambda p, c: jnp.where(column == p, ex[p], c), jnp.zeros((40, 128), F32), unroll=8)
    ez0 = lax.fori_loop(0, 128, lambda p, c: jnp.where(lane == p, ez[p], c), jnp.ones((8, 128), F32), unroll=8)
    ez1 = lax.fori_loop(0, 16, lambda p, c: jnp.where(lane == p, ez[p + 128], c), jnp.ones((8, 128), F32), unroll=8)
    ez0, ez1 = (jnp.concatenate([e] * 5, axis=0) for e in (ez0, ez1))

    def table(q, c):
        base = exc + ey[q]
        inv[0, q] = 1.0 / (base + ez0)
        inv[1, q] = 1.0 / (base + ez1)
        return c
    lax.fori_loop(0, 40, table, 0, unroll=2)

    loads[4].wait()
    RE0[pl.ds(0, 24), pl.ds(0, 24)] = rea[...]

    def zrows(b, x0, nx, t):
        for i in range(nx // 8):
            b[pl.ds(x0 + 8 * i, 8), pl.ds(t, 8)] = jnp.zeros((8, 8, 128), F32)

    for s, x0 in ((-1, 32), (1, 24)):
        @pl.when(jnp.logical_not(has_x[s]))
        def _():
            for b in (E0, RE0):
                b[pl.ds(x0, 8), pl.ds(0, 24)] = jnp.zeros((8, 24, 128), F32)
            (XL if s == -1 else XR)[...] = jnp.zeros((17, 24, 128), F32)
            X2[0 if s == -1 else 1] = jnp.zeros((8, 24, 128), F32)
    for s, t, tv in ((-1, 32, 40), (1, 24, 24)):
        @pl.when(jnp.logical_not(has_y[s]))
        def _():
            for b in (E0, RE0):
                zrows(b, 0, 40, t)
            zrows(V0, 0, 40, tv)
            V0[pl.ds(40, 2), pl.ds(tv, 8)] = jnp.zeros((2, 8, 128), F32)
            RR[0 if s == -1 else 1] = jnp.zeros((48, 128), F32)
            for b in (rmy, r2y, q2y):
                b[0 if s == -1 else 1] = jnp.zeros(b.shape[1:], F32)

    def missing(d):
        z = 0 if d[1] == 1 else 1
        y = 0 if d[0] == 1 else 1
        t, n = {0: (0, 24), 1: (32, 8), -1: (24, 8)}[d[0]]
        if d[1] == 0:
            return []
        out_ = [b.at[z, :, pl.ds(t, n)] for b in (rfA, rfB, rr)]
        if d[0] == 0:
            return out_ + [b.at[z] for b in (rmf, r2f, q2f, rvz)]
        return out_ + [b.at[y, z] for b in (rmc, r2c, q2c, rvc)]
    zero_missing(missing)

    pl.semaphore_wait(barrier, expect)

    def unpack_halo(recv, g0, groups, dst1, x0):
        def body(g, c):
            both = jnp.where(low_part(40, 16), recv[1, g], recv[0, g])
            for i in range(8):
                dst1[x0 + g * 8 + i] = edge(roll(both, -16 * i), 8)
            return c
        lax.fori_loop(g0, g0 + groups, body, 0)

    def cat3(x0, x1):
        h0, l0 = split(x0)
        h1 = x1.astype(BF16).astype(F32)
        l1 = x1 - h1
        tail = (h1 + roll(l1, 16) + roll(h1, 32)).astype(BF16)
        return jnp.concatenate([h0, l0, h0, tail], axis=1)

    def stack3(x):
        hi, lo = split(x)
        return jnp.concatenate([hi, lo, hi], axis=0)

    def forward_chunk(c, _):
        x0 = E0[pl.ds(8 * c, 8)].reshape(320, 128)
        x1 = E1[pl.ds(8 * c, 8)].reshape(320, 128)
        z = mm(cat3(x0, x1), wzf[...])
        for i in range(4):
            y = mm(wyf[:, 0:240], stack3(z[80 * i:80 * i + 80]))
            T0[pl.ds(320 * c + 80 * i, 80), :] = y[:, 0:128]
            T1[pl.ds(320 * c + 80 * i, 80), :] = y[:, 128:256]
        return _

    def middle(j, _):
        parts = []
        for i in range(2):
            q = 2 * j + i
            parts.append(jnp.concatenate([T0[pl.ds(q, 40, stride=40), :], T1[pl.ds(q, 40, stride=40), :]], axis=1))
        m = mm(wxf[:, 0:240], stack3(jnp.concatenate(parts, axis=0)))
        scale = jnp.concatenate([
            jnp.concatenate([inv[0, 2 * j + i], inv[1, 2 * j + i]], axis=1) for i in range(2)], axis=0)
        m = mm(wxb[:, 0:240], stack3(m * scale))
        for i in range(2):
            q = 2 * j + i
            T0[pl.ds(q, 40, stride=40), :] = m[40 * i:40 * i + 40, 0:128]
            T1[pl.ds(q, 40, stride=40), :] = m[40 * i:40 * i + 40, 128:256]
        return _

    def back_chunk(c, _):
        parts = []
        for i in range(4):
            x = jnp.concatenate([T0[pl.ds(320 * c + 80 * i, 80), :], T1[pl.ds(320 * c + 80 * i, 80), :]], axis=1)
            parts.append(mm(wyb[:, 0:240], stack3(x)))
        y = jnp.concatenate(parts, axis=0)
        z = mm(cat3(y[:, 0:128], y[:, 128:256]), wzb[...])
        U0[pl.ds(8 * c, 8)] = z[:, 0:128].reshape(8, 40, 128)
        U1[pl.ds(8 * c, 8)] = z[:, 128:256].reshape(8, 40, 128)
        return _

    def fold(a0, g0, groups, y0, recv_f, recv_c, recv_y):
        def body(g, c):
            both = jnp.where(low_part(24, 16), recv_f[0, g], recv_f[1, g])
            low = low_part(8, 16)
            first = jnp.where(low, recv_c[0, 0, g], recv_c[0, 1, g])
            last = jnp.where(low, recv_c[1, 0, g], recv_c[1, 1, g])
            both = both + jnp.concatenate([first, jnp.zeros((8, 128), F32), last], axis=0)
            for i in range(8):
                a = a0 + 8 * (g - g0) + i
                t = y0 + 8 * (g - g0) + i
                zpart = edge(roll(both, -16 * i), 8)
                ypart = jnp.concatenate([recv_y[0, t], jnp.zeros((8, 128), F32), recv_y[1, t]], axis=0)
                S[a] = U0[a, pl.ds(0, 24)] + (zpart + ypart)
            return c
        lax.fori_loop(g0, g0 + groups, body, 0)

    xf.start()
    fA.start()
    xf.forward()
    fA.wait()
    unpack_halo(rfA, 0, 3, E1, 0)
    lax.fori_loop(0, 3, forward_chunk, 0, unroll=UF)
    xf.wait()
    pack(pfB, lambda i: E0[24 + i, pl.ds(0, 24)], 2, 8, 16, True)
    fB.start()
    xr.start()
    fB.wait()
    unpack_halo(rfB, 0, 2, E1, 24)
    lax.fori_loop(3, 5, forward_chunk, 0, unroll=UF)
    lax.fori_loop(0, 20, middle, 0, unroll=UM)
    lax.fori_loop(0, 5, back_chunk, 0, unroll=UB)
    pack(pm, lambda i: U1[i], 5, 8, 16, False)
    m1.start()
    m1.wait()
    fold(0, 0, 5, 0, rmf, rmc, rmy)
    m2.start()
    m2.forward()

    xr.wait()
    pack(pr, lambda i: RE0[i, pl.ds(0, 24)], 5, 8, 16, True)
    rA.start()
    rA.wait()
    unpack_halo(rr, 0, 5, RE1, 0)
    m2.wait()

    def build_a(i, c):
        V0[i + 1, pl.ds(0, 24)] = S[i] + XL[i + 1]
        V0[i + 25, pl.ds(0, 24)] = S[i + 24] + XR[i]
        return c
    lax.fori_loop(0, 16, build_a, 0)
    for i in range(8):
        V0[17 + i, pl.ds(0, 24)] = S[16 + i]
    V0[0, pl.ds(0, 24)] = XL[0]
    V0[41, pl.ds(0, 24)] = XR[16]
    for s, v in ((-1, 0), (1, 33)):
        @pl.when(jnp.logical_not(has_x[s]))
        def _():
            V0[pl.ds(v, 9), pl.ds(0, 24)] = jnp.zeros((9, 24, 128), F32)
    R[...] = jnp.zeros((2, 48, 128), F32)
    for i in range(42):
        R[0, i:i + 1, :] = V0[i, 15:16, :]
        R[1, i:i + 1, :] = V0[i, 8:9, :]
    pack(pv, lambda i: V0[i, pl.ds(0, 24)], 6, 7, 18, True)
    m3.start()
    m3.wait()
    for i in range(42):
        V0[i, 39:40, :] = RR[0, i:i + 1, :]
        V0[i, 32:33, :] = RR[1, i:i + 1, :]

    def unpack_layer(g, c):
        face = jnp.where(low_part(24, 18), rvz[1, g], rvz[0, g])
        low = low_part(16, 18)
        lo_y = jnp.where(low, rvc[0, 1, g], rvc[0, 0, g])
        hi_y = jnp.where(low, rvc[1, 1, g], rvc[1, 0, g])
        between = jnp.where(sub == 0, hi_y[8:16], lo_y[0:8])
        both = jnp.concatenate([face, hi_y[0:8], between, lo_y[8:16]], axis=0)
        for i in range(7):
            V1[g * 7 + i] = edge(roll(both, -18 * i), 9)
        return c
    lax.fori_loop(0, 6, unpack_layer, 0)

    row = lax.broadcasted_iota(jnp.int32, (40, 128), 0)
    ln = lanes(40)
    inside_y = jnp.logical_not(((row >= 24) & (row < 32) & jnp.logical_not(has_y[1]))
                               | ((row >= 32) & jnp.logical_not(has_y[-1])))
    mask0 = jnp.where(inside_y, 1.0, 0.0)
    mask1 = jnp.where(inside_y & (((ln < 8) & has_z[1]) | ((ln >= 120) & has_z[-1])), 1.0, 0.0)
    ln48 = lanes(48)

    def shifts(v0, v1):
        p0, p1 = roll(v0, -1), roll(v1, -1)
        n0, n1 = roll(v0, 1), roll(v1, 1)
        top, bottom = ln48 == 127, ln48 == 0
        z0 = jnp.where(top, p1, p0) + jnp.where(bottom, n1, n0)
        z1 = jnp.where(top, p0, p1) + jnp.where(bottom, n0, n1)
        return z0 + 2.0 * v0, z1 + 2.0 * v1

    def ext(x):
        return jnp.concatenate([x[0:32], x[40:48]], axis=0)

    def level(v, c):
        A0[v], A1[v] = shifts(V0[v], V1[v])
        return c

    def stencil(a, c):
        x = jnp.where(a < 8, a + 32, a - 8)
        inside = jnp.where(((a < 8) & jnp.logical_not(has_x[-1])) | ((a >= 32) & jnp.logical_not(has_x[1])), 0.0, 1.0)
        for V, A, E, RE, m in ((V0, A0, E0, RE0, mask0), (V1, A1, E1, RE1, mask1)):
            v, z = V[a + 1], A[a + 1]
            total = A[a] + A[a + 2] + 2.0 * z
            along = 0.25 * v + 0.0625 * total
            k = 6.0 * v - 0.25 * (V[a] + V[a + 2] + z) - 0.125 * total
            k = k - (pltpu.roll(along, 47, 0) + pltpu.roll(along, 1, 0))
            E[x] = (E[x] - (RE[x] * ext(v) + ext(k))) * (m * inside)
        return c

    lax.fori_loop(0, 42, level, 0, unroll=UL)
    lax.fori_loop(0, 40, stencil, 0, unroll=US)

    lax.fori_loop(0, 5, forward_chunk, 0, unroll=UF)
    lax.fori_loop(0, 20, middle, 0, unroll=UM)
    back_chunk(0, 0)
    back_chunk(4, 0)
    pack(pl2H, lambda i: U1[jnp.where(i < 8, i, i + 24)], 2, 8, 16, False)
    l2H.start()
    lax.fori_loop(1, 4, back_chunk, 0, unroll=UB)
    pack(pl2O, lambda i: U1[i + 8], 3, 8, 16, False)
    l2O.start()
    l2H.wait()
    fold(0, 0, 1, 0, r2f, r2c, r2y)
    fold(32, 1, 1, 8, r2f, r2c, r2y)
    x2.start()
    x2.forward()
    l2O.wait()
    fold(8, 0, 3, 0, q2f, q2c, q2y)
    x2.wait()

    def finish(i, c):
        out[i] = V0[i + 9, pl.ds(0, 24)] + (S[i + 8] + X2[0, i])
        out[i + 8] = V0[i + 17, pl.ds(0, 24)] + S[i + 16]
        out[i + 16] = V0[i + 25, pl.ds(0, 24)] + (S[i + 24] + X2[1, i])
        return c
    lax.fori_loop(0, 8, finish, 0)


def solution(mesh):
    sizes = tuple(mesh.shape[a] for a in ("gx", "gy", "gz"))

    def local(right_side, reaction, basis_x, basis_y, basis_z, eigen_x, eigen_y, eigen_z):
        def vm(*shape, dtype=F32):
            return pltpu.VMEM(shape, dtype)
        scratch = [vm(24, 24, 128), vm(24, 24, 128), vm(40, 40), vm(40, 40), vm(144, 144)]
        scratch += [vm(40, 40, 128), vm(40, 40, 128), vm(40, 40, 128), vm(40, 40, 128),
                   vm(1600, 128), vm(1600, 128), vm(40, 40, 128), vm(40, 40, 128),
                   vm(42, 48, 128), vm(42, 48, 128), vm(2, 40, 40, 128), vm(40, 24, 128),
                   vm(42, 48, 128), vm(42, 48, 128),
                   vm(256, 256), vm(80, 256), vm(512, 256, dtype=BF16), vm(512, 256, dtype=BF16)]
        scratch += [vm(80, 256, dtype=BF16)] * 4
        scratch += [vm(3, 24, 128), vm(2, 24, 128), vm(5, 24, 128), vm(5, 40, 128), vm(6, 24, 128),
                    vm(2, 40, 128), vm(3, 40, 128)]
        scratch += [vm(2, 3, 40, 128), vm(2, 2, 40, 128), vm(2, 5, 40, 128),
                    vm(2, 5, 24, 128), vm(2, 2, 5, 8, 128), vm(2, 40, 8, 128),
                    vm(2, 6, 24, 128), vm(2, 2, 6, 16, 128), vm(2, 48, 128), vm(2, 48, 128),
                    vm(2, 2, 24, 128), vm(2, 2, 2, 8, 128), vm(2, 16, 8, 128),
                    vm(2, 3, 24, 128), vm(2, 2, 3, 8, 128), vm(2, 24, 8, 128),
                    vm(17, 24, 128), vm(17, 24, 128), vm(2, 8, 24, 128),
                    vm(2, 24, 128), vm(4, 24, 128), vm(2, 24, 128),
                    pltpu.SemaphoreType.DMA((120,)), pltpu.SemaphoreType.DMA((120,)), pltpu.SemaphoreType.DMA((5,))]
        vmem = pl.BlockSpec(memory_space=pltpu.VMEM)
        smem = pl.BlockSpec(memory_space=pltpu.SMEM)
        hbm = pl.BlockSpec(memory_space=pltpu.HBM)

        def body(*refs):
            kernel(sizes, *refs)

        return pl.pallas_call(
            body,
            out_shape=jax.ShapeDtypeStruct((24, 24, 128), F32),
            in_specs=[hbm] * 5 + [smem] * 3,
            out_specs=vmem,
            scratch_shapes=scratch,
            compiler_params=pltpu.CompilerParams(
                collective_id=0, has_side_effects=True, vmem_limit_bytes=60 * 1024 * 1024),
            cost_estimate=pl.CostEstimate(flops=1200000000, bytes_accessed=2000000, transcendentals=0),
        )(right_side, reaction, basis_x, basis_y, basis_z, eigen_x, eigen_y, eigen_z)

    return jax.shard_map(
        local,
        mesh=mesh,
        in_specs=(P("gx", "gy", "gz"), P("gx", "gy", "gz"), P(), P(), P(), P(), P(), P()),
        out_specs=P("gx", "gy", "gz"),
        check_vma=False,
    )
```

```python
import jax
import jax.numpy as jnp
from jax import lax
from jax.experimental import pallas as pl
from jax.experimental.pallas import tpu as pltpu
from jax.sharding import PartitionSpec as P

MESH = pl.DeviceIdType.MESH
F32 = jnp.float32
BF16 = jnp.bfloat16
DIRS = [(dy, dz) for dy in (-1, 0, 1) for dz in (-1, 0, 1) if (dy, dz) != (0, 0)]
STRAIGHT8, STRAIGHT17 = 5, 7


def split(x):
    hi = x.astype(BF16)
    return hi, (x - hi.astype(F32)).astype(BF16)


def mm(a, b):
    return lax.dot_general(a, b, (((1,), (0,)), ((), ())), preferred_element_type=F32)


def roll(x, shift):
    return pltpu.roll(x, shift % x.shape[-1], x.ndim - 1)


def kernel(sizes, f_hbm, rea_hbm, bx_hbm, by_hbm, bz_hbm, ex_hbm, ey_hbm, ez_hbm, out,
           f, rea, bx, by, bz, ex, ey, ez,
           E0, E1, RE0, RE1, T0, T1, U0, U1, V0, V1, inv, S,
           A0, A1, wz32, wxy32, wzf, wzb, wxf, wxb, wyf, wyb,
           pfA, pfB, pr, pmF, pmN, pvN, pvF, plF, plN, plO,
           rfA, rfB, rr, rmfF, rmfN, rmcF, rmcN, rmyF, rmyN, rvzN, rvzF, rvcN, rvcF, RN, RF, RRN, RRF,
           rlfF, rlfN, rlfO, rlcF, rlcN, rlcO, rlyF, rlyN, rlyO, X17, X2, RB8a, RB17, RB8b,
           ssem, rsem, lsem):
    n_gx, n_gy, n_gz = sizes
    gx, gy, gz = (lax.axis_index(a) for a in ("gx", "gy", "gz"))
    relay = n_gx == 8
    mid = n_gx // 2 - 1
    has_y = {-1: gy > 0, 0: gy >= 0, 1: gy < n_gy - 1}
    has_z = {-1: gz > 0, 0: gz >= 0, 1: gz < n_gz - 1}
    has_x = {-1: gx > 0, 1: gx < n_gx - 1}
    left = gx <= mid
    right = jnp.logical_not(left)

    def pick(a, b):
        return jnp.where(left, a, b)
    has = {d: has_y[d[0]] & has_z[d[1]] for d in DIRS}
    lane = lax.broadcasted_iota(jnp.int32, (8, 128), 1)
    sub = lax.broadcasted_iota(jnp.int32, (8, 128), 0)

    def lanes(rows):
        return lax.broadcasted_iota(jnp.int32, (rows, 128), 1)

    counter = [0]

    def slots(n):
        counter[0] += n
        return counter[0] - n

    def copy(k, src, dst, dev):
        return pltpu.make_async_remote_copy(
            src_ref=src, dst_ref=dst, send_sem=ssem.at[k], recv_sem=rsem.at[k],
            device_id=dev, device_id_type=MESH)

    class YZ:
        def __init__(self, items):
            self.items = {d: items(d) for d in DIRS}
            self.k = {d: slots(len(self.items[d])) for d in DIRS}

        def each(self, d, along):
            dev = (gx, gy + d[0], gz + d[1])
            for j, (src, dst) in enumerate(self.items[along]):
                yield copy(self.k[along] + j, src, dst, dev)

        def start(self):
            for d in DIRS:
                @pl.when(has[d])
                def _():
                    for c in self.each(d, d):
                        c.start()

        def wait(self):
            for d in DIRS:
                @pl.when(has[d])
                def _():
                    for c in self.each(d, (-d[0], -d[1])):
                        c.wait_recv()
                    for c in self.each(d, d):
                        c.wait_send()

    class XX:
        def __init__(self, srcs, dsts, layers, straight=None, rb=None):
            self.srcs, self.dsts, self.rb = srcs, dsts, rb
            self.layers, self.straight = layers, straight
            self.relayed = relay and straight is not None
            self.k = {s: slots(1) for s in (-1, 1)}
            if self.relayed:
                self.kr = slots(1)
                self.kp = {s: slots(4) for s in (-1, 1)}

        def end(self, s):
            return mid if s == 1 else mid + 1

        def via(self, s, j):
            return self.end(s) - s * j

        def whole(self, s):
            return copy(self.k[s], self.srcs[s], self.dsts[s], (gx + s, gy, gz))

        def cut(self, ref, j):
            if j == 0:
                return ref.at[pl.ds(0, self.straight)]
            return ref.at[pl.ds(self.straight, self.layers - self.straight), pl.ds(8 * (j - 1), 8)]

        def part(self, s, j):
            src = self.rb if j else self.cut(self.srcs[s], 0)
            return copy(self.kp[s] + j, src, self.cut(self.dsts[s], j), (self.end(s) + s, gy, gz))

        def leg(self, s, j):
            return pltpu.make_async_remote_copy(
                src_ref=self.cut(self.srcs[s], j), dst_ref=self.rb,
                send_sem=ssem.at[self.kp[s] + j], recv_sem=rsem.at[self.kr],
                device_id=(self.via(s, j), gy, gz), device_id_type=MESH)

        def start(self, s, cond):
            if not self.relayed:
                @pl.when(cond & has_x[s])
                def _():
                    self.whole(s).start()
                return

            @pl.when(cond & has_x[s] & (gx != self.end(s)))
            def _():
                self.whole(s).start()

            @pl.when(cond & (gx == self.end(s)))
            def _():
                for j in (1, 2, 3):
                    self.leg(s, j).start()
                self.part(s, 0).start()

        def forward(self):
            if self.relayed:
                for s in (1, -1):
                    for j in (1, 2, 3):
                        @pl.when(gx == self.via(s, j))
                        def _():
                            self.leg(s, j).wait_recv()
                            self.part(s, j).start()

        def arrive(self, s, cond):
            if not self.relayed:
                @pl.when(cond & has_x[-s])
                def _():
                    self.whole(s).wait_recv()
                return

            @pl.when(cond & has_x[-s] & (gx != self.end(s) + s))
            def _():
                self.whole(s).wait_recv()

            @pl.when(cond & (gx == self.end(s) + s))
            def _():
                for j in range(4):
                    self.part(s, j).wait_recv()

        def sent(self):
            for s in (1, -1):
                if not self.relayed:
                    @pl.when(has_x[s])
                    def _():
                        self.whole(s).wait_send()
                    continue

                @pl.when(has_x[s] & (gx != self.end(s)))
                def _():
                    self.whole(s).wait_send()

                @pl.when(gx == self.end(s))
                def _():
                    for j in (1, 2, 3):
                        self.leg(s, j).wait_send()
                    self.part(s, 0).wait_send()

                for j in (1, 2, 3):
                    @pl.when(gx == self.via(s, j))
                    def _():
                        self.part(s, j).wait_send()

        def start_far(self):
            self.start(1, left)
            self.start(-1, right)

        def start_near(self):
            self.start(-1, left)
            self.start(1, right)

        def arrive_near(self):
            self.arrive(1, left)
            self.arrive(-1, right)

        def arrive_far(self):
            self.arrive(-1, left)
            self.arrive(1, right)

    barrier = pltpu.get_barrier_semaphore()
    expect = jnp.int32(0)
    for d in DIRS:
        @pl.when(has[d])
        def _():
            pl.semaphore_signal(barrier, inc=1, device_id=(gx, gy + d[0], gz + d[1]), device_id_type=MESH)
        expect = expect + has[d].astype(jnp.int32)
    for s in (-1, 1):
        @pl.when(has_x[s])
        def _():
            pl.semaphore_signal(barrier, inc=1, device_id=(gx + s, gy, gz), device_id_type=MESH)
        expect = expect + has_x[s].astype(jnp.int32)
    if relay:
        pairs = []
        for s in (-1, 1):
            e = mid if s == 1 else mid + 1
            pairs += [(e, e - s * j) for j in (2, 3)] + [(e - s * j, e + s) for j in (1, 2, 3)]
        for a, b in pairs:
            for me, other in ((a, b), (b, a)):
                @pl.when(gx == me)
                def _():
                    pl.semaphore_signal(barrier, inc=1, device_id=(jnp.int32(other), gy, gz), device_id_type=MESH)
                expect = expect + (gx == me).astype(jnp.int32)

    loads = [pltpu.make_async_copy(a, b, lsem.at[i]) for i, (a, b) in enumerate(
        ((f_hbm, f), (bz_hbm, bz), (bx_hbm, bx), (by_hbm, by), (ex_hbm, ex), (ey_hbm, ey), (ez_hbm, ez), (rea_hbm, rea)))]
    for c in loads:
        c.start()
    for c in loads[:7]:
        c.wait()

    def edge(x, width):
        ln = lanes(x.shape[0])
        return jnp.where((ln < width) | (ln >= 128 - width), x, 0.0)

    def pack_one(dst, load, g, first, count, stride, masked):
        acc = None
        for i in range(count):
            x = load(first + i)
            if masked:
                x = edge(x, stride // 2)
            if i:
                x = roll(x, stride * i)
            acc = x if acc is None else acc + x
        dst[g] = acc

    def pack(dst, load, slabs, per, stride, masked):
        def body(g, c):
            pack_one(dst, load, g, g * per, per, stride, masked)
            return c
        full = slabs // per
        lax.fori_loop(0, full, body, 0)
        if slabs % per:
            pack_one(dst, load, full, full * per, slabs % per, stride, masked)

    def low_part(rows, stride):
        ln = lanes(rows)
        return (lax.rem(ln, stride) < stride // 2) & (ln < 128 - stride // 2 if stride == 18 else ln >= 0)

    def zero_missing(buf_of):
        for d in DIRS:
            bufs = buf_of(d)
            if bufs:
                @pl.when(jnp.logical_not(has[(-d[0], -d[1])]))
                def _():
                    for b in bufs:
                        b[...] = jnp.zeros(b.shape, F32)

    def halo_items(src, from0, x0, nx, dst, packed, recv, g0, groups):
        rows = {0: (0, 24, 0), 1: (16, 8, 32), -1: (0, 8, 24)}

        def items(d):
            s, n, t = rows[d[0]]
            if d[1] == 0:
                return [(src.at[pl.ds(from0, nx), pl.ds(s, n)], dst.at[pl.ds(x0, nx), pl.ds(t, n)])]
            return [(packed.at[pl.ds(g0, groups), pl.ds(s, n)],
                     recv.at[0 if d[1] == 1 else 1, pl.ds(g0, groups), pl.ds(t, n)])]
        return items

    def fold_items(a0, n, packed, recv_f, recv_c, recv_y):
        rows = {1: 24, -1: 32}

        def items(d):
            z = 0 if d[1] == 1 else 1
            y = 0 if d[0] == 1 else 1
            if d[1] == 0:
                return [(U0.at[pl.ds(a0, n), pl.ds(rows[d[0]], 8)], recv_y.at[y])]
            if d[0] == 0:
                return [(packed.at[:, pl.ds(0, 24)], recv_f.at[z])]
            return [(packed.at[:, pl.ds(rows[d[0]], 8)], recv_c.at[y, z])]
        return items

    def layer_items(v0, n, row_s, row_r, packed, recv_z, recv_c):
        def items(d):
            z = 0 if d[1] == 1 else 1
            y = 0 if d[0] == 1 else 1
            if d[1] == 0:
                s, t = ((16, 40), (0, 24))[y]
                return [(V0.at[pl.ds(v0, n), pl.ds(s, 8)], V0.at[pl.ds(v0, n), pl.ds(t, 8)]),
                        (row_s.at[y], row_r.at[y])]
            if d[0] == 0:
                return [(packed, recv_z.at[z])]
            return [(packed.at[:, pl.ds(8 if y == 0 else 0, 16)], recv_c.at[y, z])]
        return items

    def x_halo(b):
        return {1: b.at[pl.ds(32, 8), pl.ds(0, 24)], -1: b.at[pl.ds(24, 8), pl.ds(0, 24)]}

    def x_edge(b):
        return {1: b.at[pl.ds(16, 8)], -1: b.at[pl.ds(0, 8)]}

    xf = XX(x_edge(f), x_halo(E0), 8, STRAIGHT8, RB8a)
    xr = XX(x_edge(rea), x_halo(RE0), 8)
    xn, xfar = pick(32, 24), pick(24, 32)
    fA = YZ(halo_items(f, 0, 0, 24, E0, pfA, rfA, 0, 3))
    fN = YZ(halo_items(E0, xn, xn, 8, E0, pfB, rfB, 0, 1))
    fF = YZ(halo_items(E0, xfar, xfar, 8, E0, pfB, rfB, 1, 1))
    rA = YZ(halo_items(RE0, 0, 0, 40, RE0, pr, rr, 0, 5))
    aF, aN = pick(16, 0), pick(0, 24)
    m1F = YZ(fold_items(aF, 24, pmF, rmfF, rmcF, rmyF))
    m1N = YZ(fold_items(aN, 16, pmN, rmfN, rmcN, rmyN))
    m2 = XX({1: S.at[pl.ds(24, 17)], -1: S.at[pl.ds(1, 17)]}, {1: X17.at[0], -1: X17.at[1]}, 17, STRAIGHT17, RB17)
    vN, vF = pick(0, 17), pick(25, 0)
    m3N = YZ(layer_items(vN, 25, RN, RRN, pvN, rvzN, rvcN))
    m3F = YZ(layer_items(vF, 17, RF, RRF, pvF, rvzF, rvcF))
    eF, eN = pick(32, 0), pick(0, 32)
    l2F = YZ(fold_items(eF, 8, plF, rlfF, rlcF, rlyF))
    l2N = YZ(fold_items(eN, 8, plN, rlfN, rlcN, rlyN))
    l2O = YZ(fold_items(8, 24, plO, rlfO, rlcO, rlyO))
    x2 = XX({1: S.at[pl.ds(33, 8)], -1: S.at[pl.ds(1, 8)]}, {1: X2.at[0], -1: X2.at[1]}, 8, STRAIGHT8, RB8b)

    E0[pl.ds(0, 24), pl.ds(0, 24)] = f[...]
    pack(pfA, lambda i: f[i], 24, 8, 16, True)

    wz32[...] = jnp.zeros((256, 256), F32)
    wz32[0:128, 0:144] = bz[8:136, :]
    wz32[128:136, 0:144] = bz[136:144, :]
    wz32[248:256, 0:144] = bz[0:8, :]
    for w, table, turned in ((wzf, wz32[...], True), (wzb, wz32[...].T, False)):
        hi, lo = split(table)
        w[0:128] = hi[0:128]
        w[128:256] = hi[0:128]
        w[256:384] = lo[0:128]
        hi, lo = hi.astype(F32)[128:256], lo.astype(F32)[128:256]
        if turned:
            tail = jnp.concatenate([hi[0:8], hi[120:128], hi[0:8], lo[120:128], lo[0:8],
                                    jnp.zeros((80, 256), F32), hi[120:128]], axis=0)
        else:
            tail = jnp.concatenate([hi[0:16], hi[0:16], lo[0:16], jnp.zeros((80, 256), F32)], axis=0)
        w[384:512] = tail.astype(BF16)

    def blocks(w, m):
        wxy32[...] = jnp.zeros((80, 256), F32)
        hi, lo = split(m)
        hi, lo = hi.astype(F32), lo.astype(F32)
        for j, part in enumerate((hi, hi, lo)):
            wxy32[0:40, 80 * j:80 * j + 40] = part
            wxy32[40:80, 80 * j + 40:80 * j + 80] = part
        w[...] = wxy32[...].astype(BF16)

    x_nat, y_nat = bx[...], by[...]
    x_circ = jnp.concatenate([x_nat[8:40], x_nat[0:8]], axis=0)
    y_circ = jnp.concatenate([y_nat[8:40], y_nat[0:8]], axis=0)
    blocks(wxf, x_circ.T)
    blocks(wxb, x_nat)
    blocks(wyf, y_circ.T)
    blocks(wyb, y_circ)

    column = lax.broadcasted_iota(jnp.int32, (40, 128), 0)
    exc = lax.fori_loop(0, 40, lambda p, c: jnp.where(column == p, ex[p], c), jnp.zeros((40, 128), F32), unroll=8)
    ez0 = lax.fori_loop(0, 128, lambda p, c: jnp.where(lane == p, ez[p], c), jnp.ones((8, 128), F32), unroll=8)
    ez1 = lax.fori_loop(0, 16, lambda p, c: jnp.where(lane == p, ez[p + 128], c), jnp.ones((8, 128), F32), unroll=8)
    ez0, ez1 = (jnp.concatenate([e] * 5, axis=0) for e in (ez0, ez1))

    def table(q, c):
        base = exc + ey[q]
        inv[0, q] = 1.0 / (base + ez0)
        inv[1, q] = 1.0 / (base + ez1)
        return c
    lax.fori_loop(0, 40, table, 0, unroll=2)

    loads[7].wait()
    RE0[pl.ds(0, 24), pl.ds(0, 24)] = rea[...]

    def zrows(b, x0, nx, t):
        for i in range(nx // 8):
            b[pl.ds(x0 + 8 * i, 8), pl.ds(t, 8)] = jnp.zeros((8, 8, 128), F32)

    for s, x0 in ((-1, 32), (1, 24)):
        @pl.when(jnp.logical_not(has_x[s]))
        def _():
            for b in (E0, RE0):
                b[pl.ds(x0, 8), pl.ds(0, 24)] = jnp.zeros((8, 24, 128), F32)
            X17[0 if s == -1 else 1] = jnp.zeros((17, 24, 128), F32)
            X2[0 if s == -1 else 1] = jnp.zeros((8, 24, 128), F32)
    for s, t, tv in ((-1, 32, 40), (1, 24, 24)):
        @pl.when(jnp.logical_not(has_y[s]))
        def _():
            for b in (E0, RE0):
                zrows(b, 0, 40, t)
            zrows(V0, 0, 40, tv)
            V0[pl.ds(40, 2), pl.ds(tv, 8)] = jnp.zeros((2, 8, 128), F32)
            for b in (RRN, RRF, rmyF, rmyN, rlyF, rlyN, rlyO):
                b[0 if s == -1 else 1] = jnp.zeros(b.shape[1:], F32)

    def missing(d):
        z = 0 if d[1] == 1 else 1
        y = 0 if d[0] == 1 else 1
        t, n = {0: (0, 24), 1: (32, 8), -1: (24, 8)}[d[0]]
        if d[1] == 0:
            return []
        out_ = [b.at[z, :, pl.ds(t, n)] for b in (rfA, rfB, rr)]
        if d[0] == 0:
            return out_ + [b.at[z] for b in (rmfF, rmfN, rlfF, rlfN, rlfO, rvzN, rvzF)]
        return out_ + [b.at[y, z] for b in (rmcF, rmcN, rlcF, rlcN, rlcO, rvcN, rvcF)]
    zero_missing(missing)
    S[0] = jnp.zeros((24, 128), F32)
    S[41] = jnp.zeros((24, 128), F32)

    pl.semaphore_wait(barrier, expect)

    def unpack_group(recv, g, dst1, x0):
        both = jnp.where(low_part(40, 16), recv[1, g], recv[0, g])
        for i in range(8):
            dst1[x0 + i] = edge(roll(both, -16 * i), 8)

    def unpack_halo(recv, groups, dst1):
        def body(g, c):
            unpack_group(recv, g, dst1, 8 * g)
            return c
        lax.fori_loop(0, groups, body, 0)

    def cat3(x0, x1):
        h0, l0 = split(x0)
        h1 = x1.astype(BF16).astype(F32)
        l1 = x1 - h1
        tail = (h1 + roll(l1, 16) + roll(h1, 32)).astype(BF16)
        return jnp.concatenate([h0, l0, h0, tail], axis=1)

    def stack3(x):
        hi, lo = split(x)
        return jnp.concatenate([hi, lo, hi], axis=0)

    def forward_chunk(c, _):
        x0 = E0[pl.ds(8 * c, 8)].reshape(320, 128)
        x1 = E1[pl.ds(8 * c, 8)].reshape(320, 128)
        z = mm(cat3(x0, x1), wzf[...])
        for i in range(4):
            y = mm(wyf[:, 0:240], stack3(z[80 * i:80 * i + 80]))
            T0[pl.ds(320 * c + 80 * i, 80), :] = y[:, 0:128]
            T1[pl.ds(320 * c + 80 * i, 80), :] = y[:, 128:256]
        return _

    def middle(j, _):
        parts = []
        for i in range(2):
            q = 2 * j + i
            parts.append(jnp.concatenate([T0[pl.ds(q, 40, stride=40), :], T1[pl.ds(q, 40, stride=40), :]], axis=1))
        m = mm(wxf[:, 0:240], stack3(jnp.concatenate(parts, axis=0)))
        scale = jnp.concatenate([
            jnp.concatenate([inv[0, 2 * j + i], inv[1, 2 * j + i]], axis=1) for i in range(2)], axis=0)
        m = mm(wxb[:, 0:240], stack3(m * scale))
        for i in range(2):
            q = 2 * j + i
            T0[pl.ds(q, 40, stride=40), :] = m[40 * i:40 * i + 40, 0:128]
            T1[pl.ds(q, 40, stride=40), :] = m[40 * i:40 * i + 40, 128:256]
        return _

    def back_chunk(c, _):
        parts = []
        for i in range(4):
            x = jnp.concatenate([T0[pl.ds(320 * c + 80 * i, 80), :], T1[pl.ds(320 * c + 80 * i, 80), :]], axis=1)
            parts.append(mm(wyb[:, 0:240], stack3(x)))
        y = jnp.concatenate(parts, axis=0)
        z = mm(cat3(y[:, 0:128], y[:, 128:256]), wzb[...])
        U0[pl.ds(8 * c, 8)] = z[:, 0:128].reshape(8, 40, 128)
        U1[pl.ds(8 * c, 8)] = z[:, 128:256].reshape(8, 40, 128)
        return _

    def fold(a0, groups, recv_f, recv_c, recv_y):
        def body(g, c):
            both = jnp.where(low_part(24, 16), recv_f[0, g], recv_f[1, g])
            low = low_part(8, 16)
            first = jnp.where(low, recv_c[0, 0, g], recv_c[0, 1, g])
            last = jnp.where(low, recv_c[1, 0, g], recv_c[1, 1, g])
            both = both + jnp.concatenate([first, jnp.zeros((8, 128), F32), last], axis=0)
            for i in range(8):
                t = 8 * g + i
                zpart = edge(roll(both, -16 * i), 8)
                ypart = jnp.concatenate([recv_y[0, t], jnp.zeros((8, 128), F32), recv_y[1, t]], axis=0)
                S[a0 + t + 1] = U0[a0 + t, pl.ds(0, 24)] + (zpart + ypart)
            return c
        lax.fori_loop(0, groups, body, 0)

    def build(v0, side):
        def body(i, c):
            V0[v0 + i, pl.ds(0, 24)] = S[v0 + i] + X17[side, i]
            return c
        lax.fori_loop(0, 17, body, 0)

    def rows_out(rows, v0, n):
        rows[...] = jnp.zeros(rows.shape, F32)
        for i in range(n):
            rows[0, i:i + 1, :] = V0[v0 + i, 15:16, :]
            rows[1, i:i + 1, :] = V0[v0 + i, 8:9, :]

    def rows_in(rows, v0, n):
        for i in range(n):
            V0[v0 + i, 39:40, :] = rows[0, i:i + 1, :]
            V0[v0 + i, 32:33, :] = rows[1, i:i + 1, :]

    def unpack_layer(v0, n, recv_z, recv_c):
        def one(g, count):
            face = jnp.where(low_part(24, 18), recv_z[1, g], recv_z[0, g])
            low = low_part(16, 18)
            lo_y = jnp.where(low, recv_c[0, 1, g], recv_c[0, 0, g])
            hi_y = jnp.where(low, recv_c[1, 1, g], recv_c[1, 0, g])
            between = jnp.where(sub == 0, hi_y[8:16], lo_y[0:8])
            both = jnp.concatenate([face, hi_y[0:8], between, lo_y[8:16]], axis=0)
            for i in range(count):
                V1[v0 + g * 7 + i] = edge(roll(both, -18 * i), 9)

        def body(g, c):
            one(g, 7)
            return c
        lax.fori_loop(0, n // 7, body, 0)
        one(n // 7, n % 7)

    row = lax.broadcasted_iota(jnp.int32, (40, 128), 0)
    ln = lanes(40)
    inside_y = jnp.logical_not(((row >= 24) & (row < 32) & jnp.logical_not(has_y[1]))
                               | ((row >= 32) & jnp.logical_not(has_y[-1])))
    mask0 = jnp.where(inside_y, 1.0, 0.0)
    mask1 = jnp.where(inside_y & (((ln < 8) & has_z[1]) | ((ln >= 120) & has_z[-1])), 1.0, 0.0)
    ln48 = lanes(48)

    def shifts(v0, v1):
        p0, p1 = roll(v0, -1), roll(v1, -1)
        n0, n1 = roll(v0, 1), roll(v1, 1)
        top, bottom = ln48 == 127, ln48 == 0
        z0 = jnp.where(top, p1, p0) + jnp.where(bottom, n1, n0)
        z1 = jnp.where(top, p0, p1) + jnp.where(bottom, n0, n1)
        return z0 + 2.0 * v0, z1 + 2.0 * v1

    def ext(x):
        return jnp.concatenate([x[0:32], x[40:48]], axis=0)

    def level(v, c):
        A0[v], A1[v] = shifts(V0[v], V1[v])
        return c

    def stencil(a, c):
        x = jnp.where(a < 8, a + 32, a - 8)
        inside = jnp.where(((a < 8) & jnp.logical_not(has_x[-1])) | ((a >= 32) & jnp.logical_not(has_x[1])), 0.0, 1.0)
        for V, A, E, RE, m in ((V0, A0, E0, RE0, mask0), (V1, A1, E1, RE1, mask1)):
            v, z = V[a + 1], A[a + 1]
            total = A[a] + A[a + 2] + 2.0 * z
            along = 0.25 * v + 0.0625 * total
            k = 6.0 * v - 0.25 * (V[a] + V[a + 2] + z) - 0.125 * total
            k = k - (pltpu.roll(along, 47, 0) + pltpu.roll(along, 1, 0))
            E[x] = (E[x] - (RE[x] * ext(v) + ext(k))) * (m * inside)
        return c

    xf.start_far()
    xf.start_near()
    fA.start()
    xf.forward()
    fA.wait()
    unpack_halo(rfA, 3, E1)
    lax.fori_loop(0, 3, forward_chunk, 0, unroll=True)
    for arrive, x0, g, stage in ((xf.arrive_near, xn, 0, fN), (xf.arrive_far, xfar, 1, fF)):
        arrive()
        pack_one(pfB, lambda i: E0[x0 + i, pl.ds(0, 24)], g, 0, 8, 16, True)
        stage.start()
        if g:
            xr.start_far()
            xr.start_near()
        stage.wait()
        unpack_group(rfB, g, E1, x0)
        forward_chunk(x0 // 8, 0)
    xf.sent()
    lax.fori_loop(0, 20, middle, 0, unroll=10)
    bF, bN = pick(2, 0), pick(0, 3)
    lax.fori_loop(0, 3, lambda j, c: back_chunk(bF + j, c), 0, unroll=True)
    pack(pmF, lambda i: U1[aF + i], 24, 8, 16, False)
    m1F.start()
    lax.fori_loop(0, 2, lambda j, c: back_chunk(bN + j, c), 0, unroll=True)
    pack(pmN, lambda i: U1[aN + i], 16, 8, 16, False)
    m1N.start()
    m1F.wait()
    fold(aF, 3, rmfF, rmcF, rmyF)
    m2.start_far()
    m1N.wait()
    fold(aN, 2, rmfN, rmcN, rmyN)
    m2.start_near()
    m2.forward()

    m2.arrive_near()
    build(pick(0, 25), pick(0, 1))
    for i in range(8):
        V0[17 + i, pl.ds(0, 24)] = S[17 + i]
    for s, v in ((-1, 0), (1, 33)):
        @pl.when(jnp.logical_not(has_x[s]))
        def _():
            V0[pl.ds(v, 9), pl.ds(0, 24)] = jnp.zeros((9, 24, 128), F32)
    rows_out(RN, vN, 25)
    pack(pvN, lambda i: V0[vN + i, pl.ds(0, 24)], 25, 7, 18, True)
    m3N.start()
    xr.arrive_near()
    xr.arrive_far()
    xr.sent()
    pack(pr, lambda i: RE0[i, pl.ds(0, 24)], 40, 8, 16, True)
    rA.start()
    m3N.wait()
    rows_in(RRN, vN, 25)
    unpack_layer(vN, 25, rvzN, rvcN)
    l0 = pick(0, 18)
    lax.fori_loop(0, 24, lambda i, c: level(l0 + i, c), 0, unroll=3)
    rA.wait()
    unpack_halo(rr, 5, RE1)
    s0 = pick(0, 20)
    lax.fori_loop(0, 20, lambda i, c: stencil(s0 + i, c), 0, unroll=4)
    cN, cF = pick(0, 3), pick(2, 0)
    lax.fori_loop(0, 2, lambda j, c: forward_chunk(lax.rem(cN + j + 4, 5), c), 0, unroll=True)

    m2.arrive_far()
    m2.sent()
    build(pick(25, 0), pick(1, 0))
    rows_out(RF, vF, 17)
    pack(pvF, lambda i: V0[vF + i, pl.ds(0, 24)], 17, 7, 18, True)
    m3F.start()
    m3F.wait()
    rows_in(RRF, vF, 17)
    unpack_layer(vF, 17, rvzF, rvcF)
    l1 = pick(24, 0)
    lax.fori_loop(0, 18, lambda i, c: level(l1 + i, c), 0, unroll=3)
    s1 = pick(20, 0)
    lax.fori_loop(0, 20, lambda i, c: stencil(s1 + i, c), 0, unroll=4)

    lax.fori_loop(0, 3, lambda j, c: forward_chunk(lax.rem(cF + j + 4, 5), c), 0, unroll=True)
    lax.fori_loop(0, 20, middle, 0, unroll=10)
    for a0, packed, stage in ((eF, plF, l2F), (eN, plN, l2N)):
        back_chunk(a0 // 8, 0)
        pack_one(packed, lambda i: U1[a0 + i], 0, 0, 8, 16, False)
        stage.start()
    lax.fori_loop(1, 4, back_chunk, 0, unroll=True)
    l2F.wait()
    fold(eF, 1, rlfF, rlcF, rlyF)
    x2.start_far()
    pack(plO, lambda i: U1[i + 8], 24, 8, 16, False)
    l2O.start()
    l2N.wait()
    fold(eN, 1, rlfN, rlcN, rlyN)
    x2.start_near()
    x2.forward()
    l2O.wait()
    fold(8, 3, rlfO, rlcO, rlyO)
    x2.arrive_near()
    x2.arrive_far()
    x2.sent()

    def finish(i, c):
        out[i] = V0[i + 9, pl.ds(0, 24)] + (S[i + 9] + X2[0, i])
        out[i + 8] = V0[i + 17, pl.ds(0, 24)] + S[i + 17]
        out[i + 16] = V0[i + 25, pl.ds(0, 24)] + (S[i + 25] + X2[1, i])
        return c
    lax.fori_loop(0, 8, finish, 0)


def solution(mesh):
    sizes = tuple(mesh.shape[a] for a in ("gx", "gy", "gz"))

    def local(right_side, reaction, basis_x, basis_y, basis_z, eigen_x, eigen_y, eigen_z):
        def vm(*shape, dtype=F32):
            return pltpu.VMEM(shape, dtype)
        scratch = [vm(24, 24, 128), vm(24, 24, 128), vm(40, 40), vm(40, 40), vm(144, 144),
                   pltpu.SMEM((40,), F32), pltpu.SMEM((40,), F32), pltpu.SMEM((144,), F32)]
        scratch += [vm(40, 40, 128), vm(40, 40, 128), vm(40, 40, 128), vm(40, 40, 128),
                   vm(1600, 128), vm(1600, 128), vm(40, 40, 128), vm(40, 40, 128),
                   vm(42, 48, 128), vm(42, 48, 128), vm(2, 40, 40, 128), vm(42, 24, 128),
                   vm(42, 48, 128), vm(42, 48, 128),
                   vm(256, 256), vm(80, 256), vm(512, 256, dtype=BF16), vm(512, 256, dtype=BF16)]
        scratch += [vm(80, 256, dtype=BF16)] * 4
        scratch += [vm(3, 24, 128), vm(2, 24, 128), vm(5, 24, 128), vm(3, 40, 128), vm(2, 40, 128),
                    vm(4, 24, 128), vm(3, 24, 128), vm(1, 40, 128), vm(1, 40, 128), vm(3, 40, 128)]
        scratch += [vm(2, 3, 40, 128), vm(2, 2, 40, 128), vm(2, 5, 40, 128),
                    vm(2, 3, 24, 128), vm(2, 2, 24, 128), vm(2, 2, 3, 8, 128), vm(2, 2, 2, 8, 128),
                    vm(2, 24, 8, 128), vm(2, 16, 8, 128),
                    vm(2, 4, 24, 128), vm(2, 3, 24, 128), vm(2, 2, 4, 16, 128), vm(2, 2, 3, 16, 128),
                    vm(2, 32, 128), vm(2, 24, 128), vm(2, 32, 128), vm(2, 24, 128)]
        scratch += [vm(2, n, 24, 128) for n in (1, 1, 3)] + [vm(2, 2, n, 8, 128) for n in (1, 1, 3)]
        scratch += [vm(2, n, 8, 128) for n in (8, 8, 24)]
        scratch += [vm(2, 17, 24, 128), vm(2, 8, 24, 128),
                    vm(8 - STRAIGHT8, 8, 128), vm(17 - STRAIGHT17, 8, 128), vm(8 - STRAIGHT8, 8, 128),
                    pltpu.SemaphoreType.DMA((200,)), pltpu.SemaphoreType.DMA((200,)), pltpu.SemaphoreType.DMA((8,))]
        vmem = pl.BlockSpec(memory_space=pltpu.VMEM)
        hbm = pl.BlockSpec(memory_space=pltpu.HBM)

        def body(*refs):
            kernel(sizes, *refs)

        return pl.pallas_call(
            body,
            out_shape=jax.ShapeDtypeStruct((24, 24, 128), F32),
            in_specs=[hbm] * 8,
            out_specs=vmem,
            scratch_shapes=scratch,
            compiler_params=pltpu.CompilerParams(
                collective_id=0, has_side_effects=True, vmem_limit_bytes=40 * 1024 * 1024),
            cost_estimate=pl.CostEstimate(flops=1200000000, bytes_accessed=2000000, transcendentals=0),
        )(*(pltpu.with_memory_space_constraint(a, pltpu.HBM) for a in (
            right_side, reaction, basis_x, basis_y, basis_z, eigen_x, eigen_y, eigen_z)))

    return jax.shard_map(
        local,
        mesh=mesh,
        in_specs=(P("gx", "gy", "gz"), P("gx", "gy", "gz"), P(), P(), P(), P(), P(), P()),
        out_specs=P("gx", "gy", "gz"),
        check_vma=False,
    )
```

```python
import jax
import jax.numpy as jnp
from jax import lax
from jax.experimental import pallas as pl
from jax.experimental.pallas import tpu as pltpu
from jax.sharding import PartitionSpec as P

MESH = pl.DeviceIdType.MESH
F32 = jnp.float32
BF16 = jnp.bfloat16
DIRS = [(dy, dz) for dy in (-1, 0, 1) for dz in (-1, 0, 1) if (dy, dz) != (0, 0)]
STRAIGHT8, STRAIGHT17 = 2, 5
PIECES = 3


def split(x):
    hi = x.astype(BF16)
    return hi, (x - hi.astype(F32)).astype(BF16)


def mm(a, b):
    return lax.dot_general(a, b, (((1,), (0,)), ((), ())), preferred_element_type=F32)


def roll(x, shift):
    return pltpu.roll(x, shift % x.shape[-1], x.ndim - 1)


def kernel(sizes, f_hbm, rea_hbm, bx_hbm, by_hbm, bz_hbm, ex_hbm, ey_hbm, ez_hbm, out,
           f, rea, bx, by, bz, ex, ey, ez,
           E0, E1, RE0, RE1, T0, T1, U0, U1, V0, V1, inv, S,
           A0, A1, TP, invp, wz32, wxy32, wzf, wzb, wxf, wxb, wyf, wyb,
           pfA, pfB, pr, pmF, pmN, pvN, pvF, plF, plN, plO,
           rfA, rfB, rr, rmfF, rmfN, rmcF, rmcN, rmyF, rmyN, rvzN, rvzF, rvcN, rvcF, RN, RF, RRN, RRF,
           rlfF, rlfN, rlfO, rlcF, rlcN, rlcO, rlyF, rlyN, rlyO, X17, X2, RB8a, RB17, RB8b, RB8c,
           ssem, rsem, lsem):
    n_gx, n_gy, n_gz = sizes
    gx, gy, gz = (lax.axis_index(a) for a in ("gx", "gy", "gz"))
    relay = n_gx == 8
    mid = n_gx // 2 - 1
    has_y = {-1: gy > 0, 0: gy >= 0, 1: gy < n_gy - 1}
    has_z = {-1: gz > 0, 0: gz >= 0, 1: gz < n_gz - 1}
    has_x = {-1: gx > 0, 1: gx < n_gx - 1}
    left = gx <= mid
    right = jnp.logical_not(left)

    def pick(a, b):
        return jnp.where(left, a, b)
    has = {d: has_y[d[0]] & has_z[d[1]] for d in DIRS}
    lane = lax.broadcasted_iota(jnp.int32, (8, 128), 1)
    sub = lax.broadcasted_iota(jnp.int32, (8, 128), 0)

    def lanes(rows):
        return lax.broadcasted_iota(jnp.int32, (rows, 128), 1)

    counter = [0]

    def slots(n):
        counter[0] += n
        return counter[0] - n

    def copy(k, src, dst, dev):
        return pltpu.make_async_remote_copy(
            src_ref=src, dst_ref=dst, send_sem=ssem.at[k], recv_sem=rsem.at[k],
            device_id=dev, device_id_type=MESH)

    class YZ:
        def __init__(self, items):
            self.items = {d: items(d) for d in DIRS}
            self.k = {d: slots(len(self.items[d])) for d in DIRS}

        def each(self, d, along):
            dev = (gx, gy + d[0], gz + d[1])
            for j, (src, dst) in enumerate(self.items[along]):
                yield copy(self.k[along] + j, src, dst, dev)

        def start(self):
            for d in DIRS:
                @pl.when(has[d])
                def _():
                    for c in self.each(d, d):
                        c.start()

        def wait(self):
            for d in DIRS:
                @pl.when(has[d])
                def _():
                    for c in self.each(d, (-d[0], -d[1])):
                        c.wait_recv()
                    for c in self.each(d, d):
                        c.wait_send()

    class XX:
        def __init__(self, srcs, dsts, layers, straight=None, rb=None):
            self.srcs, self.dsts, self.rb = srcs, dsts, rb
            self.layers, self.straight = layers, straight
            self.relayed = relay and straight is not None
            self.k = {s: slots(1) for s in (-1, 1)}
            if self.relayed:
                self.kr = slots(PIECES)
                self.kp = {s: slots(1 + 3 * PIECES) for s in (-1, 1)}
                ends = [(layers - straight) * h // PIECES for h in range(PIECES + 1)]
                self.pieces = [(a, b - a) for a, b in zip(ends[:-1], ends[1:])]
                self.relays = [(j, h) for h in range(PIECES) for j in (1, 2, 3)]

        def end(self, s):
            return mid if s == 1 else mid + 1

        def via(self, s, j):
            return self.end(s) - s * j

        def whole(self, s):
            return copy(self.k[s], self.srcs[s], self.dsts[s], (gx + s, gy, gz))

        def slot(self, s, j, h):
            return self.kp[s] + (1 + 3 * h + j - 1 if j else 0)

        def cut(self, ref, j, h):
            if j == 0:
                return ref.at[pl.ds(0, self.straight)]
            lo, n = self.pieces[h]
            return ref.at[pl.ds(self.straight + lo, n), pl.ds(8 * (j - 1), 8)]

        def part(self, s, j, h=0):
            src = self.rb.at[pl.ds(*self.pieces[h])] if j else self.cut(self.srcs[s], 0, 0)
            return copy(self.slot(s, j, h), src, self.cut(self.dsts[s], j, h), (self.end(s) + s, gy, gz))

        def leg(self, s, j, h):
            return pltpu.make_async_remote_copy(
                src_ref=self.cut(self.srcs[s], j, h), dst_ref=self.rb.at[pl.ds(*self.pieces[h])],
                send_sem=ssem.at[self.slot(s, j, h)], recv_sem=rsem.at[self.kr + h],
                device_id=(self.via(s, j), gy, gz), device_id_type=MESH)

        def start(self, s, cond):
            if not self.relayed:
                @pl.when(cond & has_x[s])
                def _():
                    self.whole(s).start()
                return

            @pl.when(cond & has_x[s] & (gx != self.end(s)))
            def _():
                self.whole(s).start()

            @pl.when(cond & (gx == self.end(s)))
            def _():
                for j, h in self.relays:
                    self.leg(s, j, h).start()
                self.part(s, 0).start()

        def forward(self):
            if self.relayed:
                for s in (1, -1):
                    for j in (1, 2, 3):
                        @pl.when(gx == self.via(s, j))
                        def _():
                            for h in range(PIECES):
                                self.leg(s, j, h).wait_recv()
                                self.part(s, j, h).start()

        def arrive(self, s, cond):
            if not self.relayed:
                @pl.when(cond & has_x[-s])
                def _():
                    self.whole(s).wait_recv()
                return

            @pl.when(cond & has_x[-s] & (gx != self.end(s) + s))
            def _():
                self.whole(s).wait_recv()

            @pl.when(cond & (gx == self.end(s) + s))
            def _():
                self.part(s, 0).wait_recv()
                for j, h in self.relays:
                    self.part(s, j, h).wait_recv()

        def sent(self):
            for s in (1, -1):
                if not self.relayed:
                    @pl.when(has_x[s])
                    def _():
                        self.whole(s).wait_send()
                    continue

                @pl.when(has_x[s] & (gx != self.end(s)))
                def _():
                    self.whole(s).wait_send()

                @pl.when(gx == self.end(s))
                def _():
                    for j, h in self.relays:
                        self.leg(s, j, h).wait_send()
                    self.part(s, 0).wait_send()

                for j in (1, 2, 3):
                    @pl.when(gx == self.via(s, j))
                    def _():
                        for h in range(PIECES):
                            self.part(s, j, h).wait_send()

        def start_far(self):
            self.start(1, left)
            self.start(-1, right)

        def start_near(self):
            self.start(-1, left)
            self.start(1, right)

        def arrive_near(self):
            self.arrive(1, left)
            self.arrive(-1, right)

        def arrive_far(self):
            self.arrive(-1, left)
            self.arrive(1, right)

    barrier = pltpu.get_barrier_semaphore()
    expect = jnp.int32(0)
    for d in DIRS:
        @pl.when(has[d])
        def _():
            pl.semaphore_signal(barrier, inc=1, device_id=(gx, gy + d[0], gz + d[1]), device_id_type=MESH)
        expect = expect + has[d].astype(jnp.int32)
    for s in (-1, 1):
        @pl.when(has_x[s])
        def _():
            pl.semaphore_signal(barrier, inc=1, device_id=(gx + s, gy, gz), device_id_type=MESH)
        expect = expect + has_x[s].astype(jnp.int32)
    if relay:
        pairs = []
        for s in (-1, 1):
            e = mid if s == 1 else mid + 1
            pairs += [(e, e - s * j) for j in (2, 3)] + [(e - s * j, e + s) for j in (1, 2, 3)]
        for a, b in pairs:
            for me, other in ((a, b), (b, a)):
                @pl.when(gx == me)
                def _():
                    pl.semaphore_signal(barrier, inc=1, device_id=(jnp.int32(other), gy, gz), device_id_type=MESH)
                expect = expect + (gx == me).astype(jnp.int32)

    loads = [pltpu.make_async_copy(a, b, lsem.at[i]) for i, (a, b) in enumerate(
        ((f_hbm, f), (bz_hbm, bz), (bx_hbm, bx), (by_hbm, by), (ex_hbm, ex), (ey_hbm, ey), (ez_hbm, ez), (rea_hbm, rea)))]
    for c in loads:
        c.start()
    for c in loads[:7]:
        c.wait()

    def edge(x, width):
        ln = lanes(x.shape[0])
        return jnp.where((ln < width) | (ln >= 128 - width), x, 0.0)

    def pack_one(dst, load, g, first, count, stride, masked):
        acc = None
        for i in range(count):
            x = load(first + i)
            if masked:
                x = edge(x, stride // 2)
            if i:
                x = roll(x, stride * i)
            acc = x if acc is None else acc + x
        dst[g] = acc

    def pack(dst, load, slabs, per, stride, masked):
        def body(g, c):
            pack_one(dst, load, g, g * per, per, stride, masked)
            return c
        full = slabs // per
        lax.fori_loop(0, full, body, 0)
        if slabs % per:
            pack_one(dst, load, full, full * per, slabs % per, stride, masked)

    def low_part(rows, stride):
        ln = lanes(rows)
        return (lax.rem(ln, stride) < stride // 2) & (ln < 128 - stride // 2 if stride == 18 else ln >= 0)

    def zero_missing(buf_of):
        for d in DIRS:
            bufs = buf_of(d)
            if bufs:
                @pl.when(jnp.logical_not(has[(-d[0], -d[1])]))
                def _():
                    for b in bufs:
                        b[...] = jnp.zeros(b.shape, F32)

    def halo_items(src, from0, x0, nx, dst, packed, recv, g0, groups):
        rows = {0: (0, 24, 0), 1: (16, 8, 32), -1: (0, 8, 24)}

        def items(d):
            s, n, t = rows[d[0]]
            if d[1] == 0:
                return [(src.at[pl.ds(from0, nx), pl.ds(s, n)], dst.at[pl.ds(x0, nx), pl.ds(t, n)])]
            return [(packed.at[pl.ds(g0, groups), pl.ds(s, n)],
                     recv.at[0 if d[1] == 1 else 1, pl.ds(g0, groups), pl.ds(t, n)])]
        return items

    def fold_items(a0, n, packed, recv_f, recv_c, recv_y):
        rows = {1: 24, -1: 32}

        def items(d):
            z = 0 if d[1] == 1 else 1
            y = 0 if d[0] == 1 else 1
            if d[1] == 0:
                return [(U0.at[pl.ds(a0, n), pl.ds(rows[d[0]], 8)], recv_y.at[y])]
            if d[0] == 0:
                return [(packed.at[:, pl.ds(0, 24)], recv_f.at[z])]
            return [(packed.at[:, pl.ds(rows[d[0]], 8)], recv_c.at[y, z])]
        return items

    def layer_items(v0, n, row_s, row_r, packed, recv_z, recv_c):
        def items(d):
            z = 0 if d[1] == 1 else 1
            y = 0 if d[0] == 1 else 1
            if d[1] == 0:
                s, t = ((16, 40), (0, 24))[y]
                return [(V0.at[pl.ds(v0, n), pl.ds(s, 8)], V0.at[pl.ds(v0, n), pl.ds(t, 8)]),
                        (row_s.at[y], row_r.at[y])]
            if d[0] == 0:
                return [(packed, recv_z.at[z])]
            return [(packed.at[:, pl.ds(8 if y == 0 else 0, 16)], recv_c.at[y, z])]
        return items

    def x_halo(b):
        return {1: b.at[pl.ds(32, 8), pl.ds(0, 24)], -1: b.at[pl.ds(24, 8), pl.ds(0, 24)]}

    def x_edge(b):
        return {1: b.at[pl.ds(16, 8)], -1: b.at[pl.ds(0, 8)]}

    xf = XX(x_edge(f), x_halo(E0), 8, STRAIGHT8, RB8a)
    xr = XX(x_edge(rea), x_halo(RE0), 8, STRAIGHT8, RB8c)
    xn, xfar = pick(32, 24), pick(24, 32)
    fA = YZ(halo_items(f, 0, 0, 24, E0, pfA, rfA, 0, 3))
    fN = YZ(halo_items(E0, xn, xn, 8, E0, pfB, rfB, 0, 1))
    fF = YZ(halo_items(E0, xfar, xfar, 8, E0, pfB, rfB, 1, 1))
    rA = YZ(halo_items(RE0, 0, 0, 40, RE0, pr, rr, 0, 5))
    aF, aN = pick(16, 0), pick(0, 24)
    m1F = YZ(fold_items(aF, 24, pmF, rmfF, rmcF, rmyF))
    m1N = YZ(fold_items(aN, 16, pmN, rmfN, rmcN, rmyN))
    m2 = XX({1: S.at[pl.ds(24, 17)], -1: S.at[pl.ds(1, 17)]}, {1: X17.at[0], -1: X17.at[1]}, 17, STRAIGHT17, RB17)
    vN, vF = pick(0, 17), pick(25, 0)
    m3N = YZ(layer_items(vN, 25, RN, RRN, pvN, rvzN, rvcN))
    m3F = YZ(layer_items(vF, 17, RF, RRF, pvF, rvzF, rvcF))
    eF, eN = pick(32, 0), pick(0, 32)
    l2F = YZ(fold_items(eF, 8, plF, rlfF, rlcF, rlyF))
    l2N = YZ(fold_items(eN, 8, plN, rlfN, rlcN, rlyN))
    l2O = YZ(fold_items(8, 24, plO, rlfO, rlcO, rlyO))
    x2 = XX({1: S.at[pl.ds(33, 8)], -1: S.at[pl.ds(1, 8)]}, {1: X2.at[0], -1: X2.at[1]}, 8, STRAIGHT8, RB8b)

    E0[pl.ds(0, 24), pl.ds(0, 24)] = f[...]
    pack(pfA, lambda i: f[i], 24, 8, 16, True)

    wz32[...] = jnp.zeros((256, 256), F32)
    wz32[0:128, 0:144] = bz[8:136, :]
    wz32[128:136, 0:144] = bz[136:144, :]
    wz32[248:256, 0:144] = bz[0:8, :]
    for w, table, turned in ((wzf, wz32[...], True), (wzb, wz32[...].T, False)):
        hi, lo = split(table)
        w[0:128] = hi[0:128]
        w[128:256] = hi[0:128]
        w[256:384] = lo[0:128]
        hi, lo = hi.astype(F32)[128:256], lo.astype(F32)[128:256]
        if turned:
            tail = jnp.concatenate([hi[0:8], hi[120:128], hi[0:8], lo[120:128], lo[0:8],
                                    jnp.zeros((80, 256), F32), hi[120:128]], axis=0)
        else:
            tail = jnp.concatenate([hi[0:16], hi[0:16], lo[0:16], jnp.zeros((80, 256), F32)], axis=0)
        w[384:512] = tail.astype(BF16)

    def blocks(w, m):
        wxy32[...] = jnp.zeros((80, 256), F32)
        hi, lo = split(m)
        hi, lo = hi.astype(F32), lo.astype(F32)
        for j, part in enumerate((hi, hi, lo)):
            wxy32[0:40, 80 * j:80 * j + 40] = part
            wxy32[40:80, 80 * j + 40:80 * j + 80] = part
        w[...] = wxy32[...].astype(BF16)

    x_nat, y_nat = bx[...], by[...]
    x_circ = jnp.concatenate([x_nat[8:40], x_nat[0:8]], axis=0)
    y_circ = jnp.concatenate([y_nat[8:40], y_nat[0:8]], axis=0)
    blocks(wxf, x_circ.T)
    blocks(wxb, x_nat)
    blocks(wyf, y_circ.T)
    blocks(wyb, y_circ)

    column = lax.broadcasted_iota(jnp.int32, (40, 128), 0)
    exc = lax.fori_loop(0, 40, lambda p, c: jnp.where(column == p, ex[p], c), jnp.zeros((40, 128), F32), unroll=8)
    ez0 = lax.fori_loop(0, 128, lambda p, c: jnp.where(lane == p, ez[p], c), jnp.ones((8, 128), F32), unroll=8)
    ez1 = lax.fori_loop(0, 16, lambda p, c: jnp.where(lane == p, ez[p + 128], c), jnp.ones((8, 128), F32), unroll=8)
    ez0, ez1 = (jnp.concatenate([e] * 5, axis=0) for e in (ez0, ez1))

    first16 = lanes(40) < 16

    def table(g, c):
        acc = None
        for i in range(8):
            base = exc + ey[8 * g + i]
            inv[8 * g + i] = 1.0 / (base + ez0)
            tail = jnp.where(first16, 1.0 / (base + ez1), 0.0)
            acc = tail if acc is None else acc + roll(tail, 16 * i)
        invp[g] = acc
        return c
    lax.fori_loop(0, 5, table, 0)
    invp[5] = jnp.zeros((40, 128), F32)
    TP[5] = jnp.zeros((40, 128), F32)

    loads[7].wait()
    RE0[pl.ds(0, 24), pl.ds(0, 24)] = rea[...]

    def zrows(b, x0, nx, t):
        for i in range(nx // 8):
            b[pl.ds(x0 + 8 * i, 8), pl.ds(t, 8)] = jnp.zeros((8, 8, 128), F32)

    for s, x0 in ((-1, 32), (1, 24)):
        @pl.when(jnp.logical_not(has_x[s]))
        def _():
            for b in (E0, RE0):
                b[pl.ds(x0, 8), pl.ds(0, 24)] = jnp.zeros((8, 24, 128), F32)
            X17[0 if s == -1 else 1] = jnp.zeros((17, 24, 128), F32)
            X2[0 if s == -1 else 1] = jnp.zeros((8, 24, 128), F32)
    for s, t, tv in ((-1, 32, 40), (1, 24, 24)):
        @pl.when(jnp.logical_not(has_y[s]))
        def _():
            for b in (E0, RE0):
                zrows(b, 0, 40, t)
            zrows(V0, 0, 40, tv)
            V0[pl.ds(40, 2), pl.ds(tv, 8)] = jnp.zeros((2, 8, 128), F32)
            for b in (RRN, RRF, rmyF, rmyN, rlyF, rlyN, rlyO):
                b[0 if s == -1 else 1] = jnp.zeros(b.shape[1:], F32)

    def missing(d):
        z = 0 if d[1] == 1 else 1
        y = 0 if d[0] == 1 else 1
        t, n = {0: (0, 24), 1: (32, 8), -1: (24, 8)}[d[0]]
        if d[1] == 0:
            return []
        out_ = [b.at[z, :, pl.ds(t, n)] for b in (rfA, rfB, rr)]
        if d[0] == 0:
            return out_ + [b.at[z] for b in (rmfF, rmfN, rlfF, rlfN, rlfO, rvzN, rvzF)]
        return out_ + [b.at[y, z] for b in (rmcF, rmcN, rlcF, rlcN, rlcO, rvcN, rvcF)]
    zero_missing(missing)
    S[0] = jnp.zeros((24, 128), F32)
    S[41] = jnp.zeros((24, 128), F32)

    pl.semaphore_wait(barrier, expect)

    def unpack_group(recv, g, dst1, x0):
        both = jnp.where(low_part(40, 16), recv[1, g], recv[0, g])
        for i in range(8):
            dst1[x0 + i] = edge(roll(both, -16 * i), 8)

    def unpack_halo(recv, groups, dst1):
        def body(g, c):
            unpack_group(recv, g, dst1, 8 * g)
            return c
        lax.fori_loop(0, groups, body, 0)

    def cat3(x0, x1):
        h0, l0 = split(x0)
        h1 = x1.astype(BF16).astype(F32)
        l1 = x1 - h1
        tail = (h1 + roll(l1, 16) + roll(h1, 32)).astype(BF16)
        return jnp.concatenate([h0, l0, h0, tail], axis=1)

    def stack3(x):
        hi, lo = split(x)
        return jnp.concatenate([hi, lo, hi], axis=0)

    def forward_chunk(c, _):
        x0 = E0[pl.ds(8 * c, 8)].reshape(320, 128)
        x1 = E1[pl.ds(8 * c, 8)].reshape(320, 128)
        z = mm(cat3(x0, x1), wzf[...])
        for i in range(4):
            y = mm(wyf[:, 0:240], stack3(z[80 * i:80 * i + 80]))
            T0[pl.ds(320 * c + 80 * i, 80), :] = y[:, 0:128]
            T1[pl.ds(320 * c + 80 * i, 80), :] = y[:, 128:256]
        return _

    def four(load):
        x = [load(i) for i in range(4)]
        return jnp.concatenate([jnp.concatenate(x[0:2], axis=0), jnp.concatenate(x[2:4], axis=0)], axis=1)

    def divide(x, scale):
        m = mm(wxf[:, 0:240], stack3(x))
        m = mm(wxb[:, 0:240], stack3(m * scale))
        return [m[40 * (i % 2):40 * (i % 2) + 40, 128 * (i // 2):128 * (i // 2) + 128] for i in range(4)]

    def middle():
        def at(q):
            return pl.ds(q, 40, stride=40)

        def group(g, c):
            acc = None
            for i in range(8):
                t = T1[at(8 * g + i), :]
                acc = t if acc is None else acc + roll(t, 16 * i)
            TP[g] = acc
            for h in range(2):
                q = 8 * g + 4 * h
                for i, m in enumerate(divide(four(lambda i: T0[at(q + i), :]), four(lambda i: inv[q + i]))):
                    T0[at(q + i), :] = m
            return c
        lax.fori_loop(0, 5, group, 0, unroll=True)
        tails = divide(four(lambda i: TP[i]), four(lambda i: invp[i]))
        tails += divide(four(lambda i: TP[4 if i == 0 else 5]), four(lambda i: invp[4 if i == 0 else 5]))[0:1]
        for g in range(5):
            for i in range(8):
                T1[at(8 * g + i), :] = jnp.where(first16, roll(tails[g], -16 * i), 0.0)

    def back_chunk(c, _):
        parts = []
        for i in range(4):
            x = jnp.concatenate([T0[pl.ds(320 * c + 80 * i, 80), :], T1[pl.ds(320 * c + 80 * i, 80), :]], axis=1)
            parts.append(mm(wyb[:, 0:240], stack3(x)))
        y = jnp.concatenate(parts, axis=0)
        z = mm(cat3(y[:, 0:128], y[:, 128:256]), wzb[...])
        U0[pl.ds(8 * c, 8)] = z[:, 0:128].reshape(8, 40, 128)
        U1[pl.ds(8 * c, 8)] = z[:, 128:256].reshape(8, 40, 128)
        return _

    def fold(a0, groups, recv_f, recv_c, recv_y):
        def body(g, c):
            both = jnp.where(low_part(24, 16), recv_f[0, g], recv_f[1, g])
            low = low_part(8, 16)
            first = jnp.where(low, recv_c[0, 0, g], recv_c[0, 1, g])
            last = jnp.where(low, recv_c[1, 0, g], recv_c[1, 1, g])
            both = both + jnp.concatenate([first, jnp.zeros((8, 128), F32), last], axis=0)
            for i in range(8):
                t = 8 * g + i
                zpart = edge(roll(both, -16 * i), 8)
                ypart = jnp.concatenate([recv_y[0, t], jnp.zeros((8, 128), F32), recv_y[1, t]], axis=0)
                S[a0 + t + 1] = U0[a0 + t, pl.ds(0, 24)] + (zpart + ypart)
            return c
        lax.fori_loop(0, groups, body, 0)

    def build(v0, side):
        def body(i, c):
            V0[v0 + i, pl.ds(0, 24)] = S[v0 + i] + X17[side, i]
            return c
        lax.fori_loop(0, 17, body, 0)

    def rows_out(rows, v0, n):
        rows[...] = jnp.zeros(rows.shape, F32)
        for i in range(n):
            rows[0, i:i + 1, :] = V0[v0 + i, 15:16, :]
            rows[1, i:i + 1, :] = V0[v0 + i, 8:9, :]

    def rows_in(rows, v0, n):
        for i in range(n):
            V0[v0 + i, 39:40, :] = rows[0, i:i + 1, :]
            V0[v0 + i, 32:33, :] = rows[1, i:i + 1, :]

    def unpack_layer(v0, n, recv_z, recv_c):
        def one(g, count):
            face = jnp.where(low_part(24, 18), recv_z[1, g], recv_z[0, g])
            low = low_part(16, 18)
            lo_y = jnp.where(low, recv_c[0, 1, g], recv_c[0, 0, g])
            hi_y = jnp.where(low, recv_c[1, 1, g], recv_c[1, 0, g])
            between = jnp.where(sub == 0, hi_y[8:16], lo_y[0:8])
            both = jnp.concatenate([face, hi_y[0:8], between, lo_y[8:16]], axis=0)
            for i in range(count):
                V1[v0 + g * 7 + i] = edge(roll(both, -18 * i), 9)

        def body(g, c):
            one(g, 7)
            return c
        lax.fori_loop(0, n // 7, body, 0)
        one(n // 7, n % 7)

    row = lax.broadcasted_iota(jnp.int32, (40, 128), 0)
    ln = lanes(40)
    inside_y = jnp.logical_not(((row >= 24) & (row < 32) & jnp.logical_not(has_y[1]))
                               | ((row >= 32) & jnp.logical_not(has_y[-1])))
    mask0 = jnp.where(inside_y, 1.0, 0.0)
    mask1 = jnp.where(inside_y & (((ln < 8) & has_z[1]) | ((ln >= 120) & has_z[-1])), 1.0, 0.0)
    ln48 = lanes(48)

    def shifts(v0, v1):
        p0, p1 = roll(v0, -1), roll(v1, -1)
        n0, n1 = roll(v0, 1), roll(v1, 1)
        top, bottom = ln48 == 127, ln48 == 0
        z0 = jnp.where(top, p1, p0) + jnp.where(bottom, n1, n0)
        z1 = jnp.where(top, p0, p1) + jnp.where(bottom, n0, n1)
        return z0 + 2.0 * v0, z1 + 2.0 * v1

    def ext(x):
        return jnp.concatenate([x[0:32], x[40:48]], axis=0)

    def level(v, c):
        A0[v], A1[v] = shifts(V0[v], V1[v])
        return c

    def stencil(a, c):
        x = jnp.where(a < 8, a + 32, a - 8)
        inside = jnp.where(((a < 8) & jnp.logical_not(has_x[-1])) | ((a >= 32) & jnp.logical_not(has_x[1])), 0.0, 1.0)
        for V, A, E, RE, m in ((V0, A0, E0, RE0, mask0), (V1, A1, E1, RE1, mask1)):
            v, z = V[a + 1], A[a + 1]
            total = A[a] + A[a + 2] + 2.0 * z
            along = 0.25 * v + 0.0625 * total
            k = 6.0 * v - 0.25 * (V[a] + V[a + 2] + z) - 0.125 * total
            k = k - (pltpu.roll(along, 47, 0) + pltpu.roll(along, 1, 0))
            E[x] = (E[x] - (RE[x] * ext(v) + ext(k))) * (m * inside)
        return c

    xf.start_far()
    xf.start_near()
    fA.start()
    xf.forward()
    fA.wait()
    unpack_halo(rfA, 3, E1)
    lax.fori_loop(0, 3, forward_chunk, 0, unroll=True)
    for arrive, x0, g, stage in ((xf.arrive_near, xn, 0, fN), (xf.arrive_far, xfar, 1, fF)):
        arrive()
        pack_one(pfB, lambda i: E0[x0 + i, pl.ds(0, 24)], g, 0, 8, 16, True)
        stage.start()
        if g:
            xr.start_far()
            xr.start_near()
        stage.wait()
        unpack_group(rfB, g, E1, x0)
        forward_chunk(x0 // 8, 0)
    xf.sent()
    middle()
    bF, bN = pick(2, 0), pick(0, 3)
    lax.fori_loop(0, 3, lambda j, c: back_chunk(bF + j, c), 0, unroll=True)
    pack(pmF, lambda i: U1[aF + i], 24, 8, 16, False)
    m1F.start()
    lax.fori_loop(0, 2, lambda j, c: back_chunk(bN + j, c), 0, unroll=True)
    pack(pmN, lambda i: U1[aN + i], 16, 8, 16, False)
    m1N.start()
    xr.forward()
    m1F.wait()
    fold(aF, 3, rmfF, rmcF, rmyF)
    m2.start_far()
    m1N.wait()
    fold(aN, 2, rmfN, rmcN, rmyN)
    m2.start_near()
    m2.forward()

    m2.arrive_near()
    build(pick(0, 25), pick(0, 1))
    for i in range(8):
        V0[17 + i, pl.ds(0, 24)] = S[17 + i]
    for s, v in ((-1, 0), (1, 33)):
        @pl.when(jnp.logical_not(has_x[s]))
        def _():
            V0[pl.ds(v, 9), pl.ds(0, 24)] = jnp.zeros((9, 24, 128), F32)
    rows_out(RN, vN, 25)
    pack(pvN, lambda i: V0[vN + i, pl.ds(0, 24)], 25, 7, 18, True)
    m3N.start()
    xr.arrive_near()
    xr.arrive_far()
    xr.sent()
    pack(pr, lambda i: RE0[i, pl.ds(0, 24)], 40, 8, 16, True)
    rA.start()
    m3N.wait()
    rows_in(RRN, vN, 25)
    unpack_layer(vN, 25, rvzN, rvcN)
    l0 = pick(0, 18)
    lax.fori_loop(0, 24, lambda i, c: level(l0 + i, c), 0, unroll=3)
    rA.wait()
    unpack_halo(rr, 5, RE1)
    s0 = pick(0, 20)
    lax.fori_loop(0, 20, lambda i, c: stencil(s0 + i, c), 0, unroll=4)
    cN, cF = pick(0, 3), pick(2, 0)
    lax.fori_loop(0, 2, lambda j, c: forward_chunk(lax.rem(cN + j + 4, 5), c), 0, unroll=True)

    m2.arrive_far()
    m2.sent()
    build(pick(25, 0), pick(1, 0))
    rows_out(RF, vF, 17)
    pack(pvF, lambda i: V0[vF + i, pl.ds(0, 24)], 17, 7, 18, True)
    m3F.start()
    m3F.wait()
    rows_in(RRF, vF, 17)
    unpack_layer(vF, 17, rvzF, rvcF)
    l1 = pick(24, 0)
    lax.fori_loop(0, 18, lambda i, c: level(l1 + i, c), 0, unroll=3)
    s1 = pick(20, 0)
    lax.fori_loop(0, 20, lambda i, c: stencil(s1 + i, c), 0, unroll=4)

    lax.fori_loop(0, 3, lambda j, c: forward_chunk(lax.rem(cF + j + 4, 5), c), 0, unroll=True)
    middle()
    for a0, packed, stage in ((eF, plF, l2F), (eN, plN, l2N)):
        back_chunk(a0 // 8, 0)
        pack_one(packed, lambda i: U1[a0 + i], 0, 0, 8, 16, False)
        stage.start()
    lax.fori_loop(1, 4, back_chunk, 0, unroll=True)
    l2F.wait()
    fold(eF, 1, rlfF, rlcF, rlyF)
    x2.start_far()
    pack(plO, lambda i: U1[i + 8], 24, 8, 16, False)
    l2O.start()
    l2N.wait()
    fold(eN, 1, rlfN, rlcN, rlyN)
    x2.start_near()
    x2.forward()
    l2O.wait()
    fold(8, 3, rlfO, rlcO, rlyO)
    x2.arrive_near()
    x2.arrive_far()
    x2.sent()

    def finish(i, c):
        out[i] = V0[i + 9, pl.ds(0, 24)] + (S[i + 9] + X2[0, i])
        out[i + 8] = V0[i + 17, pl.ds(0, 24)] + S[i + 17]
        out[i + 16] = V0[i + 25, pl.ds(0, 24)] + (S[i + 25] + X2[1, i])
        return c
    lax.fori_loop(0, 8, finish, 0)


def solution(mesh):
    sizes = tuple(mesh.shape[a] for a in ("gx", "gy", "gz"))

    def local(right_side, reaction, basis_x, basis_y, basis_z, eigen_x, eigen_y, eigen_z):
        def vm(*shape, dtype=F32):
            return pltpu.VMEM(shape, dtype)
        scratch = [vm(24, 24, 128), vm(24, 24, 128), vm(40, 40), vm(40, 40), vm(144, 144),
                   pltpu.SMEM((40,), F32), pltpu.SMEM((40,), F32), pltpu.SMEM((144,), F32)]
        scratch += [vm(40, 40, 128), vm(40, 40, 128), vm(40, 40, 128), vm(40, 40, 128),
                   vm(1600, 128), vm(1600, 128), vm(40, 40, 128), vm(40, 40, 128),
                   vm(42, 48, 128), vm(42, 48, 128), vm(40, 40, 128), vm(42, 24, 128),
                   vm(42, 48, 128), vm(42, 48, 128), vm(6, 40, 128), vm(6, 40, 128),
                   vm(256, 256), vm(80, 256), vm(512, 256, dtype=BF16), vm(512, 256, dtype=BF16)]
        scratch += [vm(80, 256, dtype=BF16)] * 4
        scratch += [vm(3, 24, 128), vm(2, 24, 128), vm(5, 24, 128), vm(3, 40, 128), vm(2, 40, 128),
                    vm(4, 24, 128), vm(3, 24, 128), vm(1, 40, 128), vm(1, 40, 128), vm(3, 40, 128)]
        scratch += [vm(2, 3, 40, 128), vm(2, 2, 40, 128), vm(2, 5, 40, 128),
                    vm(2, 3, 24, 128), vm(2, 2, 24, 128), vm(2, 2, 3, 8, 128), vm(2, 2, 2, 8, 128),
                    vm(2, 24, 8, 128), vm(2, 16, 8, 128),
                    vm(2, 4, 24, 128), vm(2, 3, 24, 128), vm(2, 2, 4, 16, 128), vm(2, 2, 3, 16, 128),
                    vm(2, 32, 128), vm(2, 24, 128), vm(2, 32, 128), vm(2, 24, 128)]
        scratch += [vm(2, n, 24, 128) for n in (1, 1, 3)] + [vm(2, 2, n, 8, 128) for n in (1, 1, 3)]
        scratch += [vm(2, n, 8, 128) for n in (8, 8, 24)]
        scratch += [vm(2, 17, 24, 128), vm(2, 8, 24, 128),
                    vm(8 - STRAIGHT8, 8, 128), vm(17 - STRAIGHT17, 8, 128), vm(8 - STRAIGHT8, 8, 128), vm(8 - STRAIGHT8, 8, 128),
                    pltpu.SemaphoreType.DMA((240,)), pltpu.SemaphoreType.DMA((240,)), pltpu.SemaphoreType.DMA((8,))]
        vmem = pl.BlockSpec(memory_space=pltpu.VMEM)
        hbm = pl.BlockSpec(memory_space=pltpu.HBM)

        def body(*refs):
            kernel(sizes, *refs)

        return pl.pallas_call(
            body,
            out_shape=jax.ShapeDtypeStruct((24, 24, 128), F32),
            in_specs=[hbm] * 8,
            out_specs=vmem,
            scratch_shapes=scratch,
            compiler_params=pltpu.CompilerParams(
                collective_id=0, has_side_effects=True, vmem_limit_bytes=40 * 1024 * 1024),
            cost_estimate=pl.CostEstimate(flops=1200000000, bytes_accessed=2000000, transcendentals=0),
        )(*(pltpu.with_memory_space_constraint(a, pltpu.HBM) for a in (
            right_side, reaction, basis_x, basis_y, basis_z, eigen_x, eigen_y, eigen_z)))

    return jax.shard_map(
        local,
        mesh=mesh,
        in_specs=(P("gx", "gy", "gz"), P("gx", "gy", "gz"), P(), P(), P(), P(), P(), P()),
        out_specs=P("gx", "gy", "gz"),
        check_vma=False,
    )
```

```python
import jax
import jax.numpy as jnp
from jax import lax
from jax.experimental import pallas as pl
from jax.experimental.pallas import tpu as pltpu
from jax.sharding import PartitionSpec as P

MESH = pl.DeviceIdType.MESH
F32 = jnp.float32
BF16 = jnp.bfloat16
DIRS = [(-1, 0), (1, 0), (0, -1), (0, 1), (-1, -1), (-1, 1), (1, -1), (1, 1)]
STRAIGHT8, STRAIGHT16 = 3, 5
PIECES = 3


def split(x):
    hi = x.astype(BF16)
    return hi, (x - hi.astype(F32)).astype(BF16)


def mm(a, b):
    return lax.dot_general(a, b, (((1,), (0,)), ((), ())), preferred_element_type=F32)


def roll(x, shift):
    return pltpu.roll(x, shift % x.shape[-1], x.ndim - 1)


def kernel(sizes, f_hbm, rea_hbm, bx_hbm, by_hbm, bz_hbm, ex_hbm, ey_hbm, ez_hbm, out,
           f, rea, bx, by, bz, ex, ey, ez,
           E0, E1, RE0, RE1, T0, T1, U0, U1, V0, V1, inv, S,
           A0, A1, TP, invp, wz32, wxy32, wzf, wzb, wxf, wxb, wyf, wyb,
           pfA, pfB, pr, pmF, pmN, pvN, pvF, plF, plN, plO,
           rfA, rfB, rr, rmfF, rmfN, rmcF, rmcN, rmyF, rmyN, rvzN, rvzF, rvcN, rvcF, RN, RF, RRN, RRF,
           rlfF, rlfN, rlfO, rlcF, rlcN, rlcO, rlyF, rlyN, rlyO, X17, X2, RB8a, RB16, RB8b, RB8c,
           ssem, rsem, lsem):
    n_gx, n_gy, n_gz = sizes
    gx, gy, gz = (lax.axis_index(a) for a in ("gx", "gy", "gz"))
    relay = n_gx == 8
    mid = n_gx // 2 - 1
    has_y = {-1: gy > 0, 0: gy >= 0, 1: gy < n_gy - 1}
    has_z = {-1: gz > 0, 0: gz >= 0, 1: gz < n_gz - 1}
    has_x = {-1: gx > 0, 1: gx < n_gx - 1}
    left = gx <= mid
    right = jnp.logical_not(left)

    def pick(a, b):
        return jnp.where(left, a, b)
    has = {d: has_y[d[0]] & has_z[d[1]] for d in DIRS}
    lane = lax.broadcasted_iota(jnp.int32, (8, 128), 1)
    sub = lax.broadcasted_iota(jnp.int32, (8, 128), 0)

    def lanes(rows):
        return lax.broadcasted_iota(jnp.int32, (rows, 128), 1)

    counter = [0]

    def slots(n):
        counter[0] += n
        return counter[0] - n

    def copy(k, src, dst, dev):
        return pltpu.make_async_remote_copy(
            src_ref=src, dst_ref=dst, send_sem=ssem.at[k], recv_sem=rsem.at[k],
            device_id=dev, device_id_type=MESH)

    class YZ:
        def __init__(self, items):
            self.items = {d: items(d) for d in DIRS}
            self.k = {d: slots(len(self.items[d])) for d in DIRS}

        def each(self, d, along):
            dev = (gx, gy + d[0], gz + d[1])
            for j, (src, dst) in enumerate(self.items[along]):
                yield copy(self.k[along] + j, src, dst, dev)

        def start(self):
            for d in DIRS:
                @pl.when(has[d])
                def _():
                    for c in self.each(d, d):
                        c.start()

        def arrive(self):
            for d in DIRS:
                @pl.when(has[d])
                def _():
                    for c in self.each(d, (-d[0], -d[1])):
                        c.wait_recv()

        def sent(self):
            for d in DIRS:
                @pl.when(has[d])
                def _():
                    for c in self.each(d, d):
                        c.wait_send()

    class XX:
        def __init__(self, srcs, dsts, layers, straight=None, rb=None):
            self.srcs, self.dsts, self.rb = srcs, dsts, rb
            self.layers, self.straight = layers, straight
            self.relayed = relay and straight is not None
            self.k = {s: slots(1) for s in (-1, 1)}
            if self.relayed:
                self.kr = slots(PIECES)
                self.kp = {s: slots(1 + 3 * PIECES) for s in (-1, 1)}
                ends = [(layers - straight) * h // PIECES for h in range(PIECES + 1)]
                self.pieces = [(a, b - a) for a, b in zip(ends[:-1], ends[1:])]
                self.relays = [(j, h) for h in range(PIECES) for j in (1, 2, 3)]

        def end(self, s):
            return mid if s == 1 else mid + 1

        def via(self, s, j):
            return self.end(s) - s * j

        def whole(self, s):
            return copy(self.k[s], self.srcs[s], self.dsts[s], (gx + s, gy, gz))

        def slot(self, s, j, h):
            return self.kp[s] + (1 + 3 * h + j - 1 if j else 0)

        def cut(self, ref, j, h):
            if j == 0:
                return ref.at[pl.ds(0, self.straight)]
            lo, n = self.pieces[h]
            return ref.at[pl.ds(self.straight + lo, n), pl.ds(8 * (j - 1), 8)]

        def part(self, s, j, h=0):
            src = self.rb.at[pl.ds(*self.pieces[h])] if j else self.cut(self.srcs[s], 0, 0)
            return copy(self.slot(s, j, h), src, self.cut(self.dsts[s], j, h), (self.end(s) + s, gy, gz))

        def leg(self, s, j, h):
            return pltpu.make_async_remote_copy(
                src_ref=self.cut(self.srcs[s], j, h), dst_ref=self.rb.at[pl.ds(*self.pieces[h])],
                send_sem=ssem.at[self.slot(s, j, h)], recv_sem=rsem.at[self.kr + h],
                device_id=(self.via(s, j), gy, gz), device_id_type=MESH)

        def start(self, s, cond):
            if not self.relayed:
                @pl.when(cond & has_x[s])
                def _():
                    self.whole(s).start()
                return

            @pl.when(cond & has_x[s] & (gx != self.end(s)))
            def _():
                self.whole(s).start()

            @pl.when(cond & (gx == self.end(s)))
            def _():
                for j, h in self.relays:
                    self.leg(s, j, h).start()
                self.part(s, 0).start()

        def forward(self):
            if self.relayed:
                for s in (1, -1):
                    for j in (1, 2, 3):
                        @pl.when(gx == self.via(s, j))
                        def _():
                            for h in range(PIECES):
                                self.leg(s, j, h).wait_recv()
                                self.part(s, j, h).start()

        def arrive(self, s, cond):
            if not self.relayed:
                @pl.when(cond & has_x[-s])
                def _():
                    self.whole(s).wait_recv()
                return

            @pl.when(cond & has_x[-s] & (gx != self.end(s) + s))
            def _():
                self.whole(s).wait_recv()

            @pl.when(cond & (gx == self.end(s) + s))
            def _():
                self.part(s, 0).wait_recv()
                for j, h in self.relays:
                    self.part(s, j, h).wait_recv()

        def sent(self):
            for s in (1, -1):
                if not self.relayed:
                    @pl.when(has_x[s])
                    def _():
                        self.whole(s).wait_send()
                    continue

                @pl.when(has_x[s] & (gx != self.end(s)))
                def _():
                    self.whole(s).wait_send()

                @pl.when(gx == self.end(s))
                def _():
                    for j, h in self.relays:
                        self.leg(s, j, h).wait_send()
                    self.part(s, 0).wait_send()

                for j in (1, 2, 3):
                    @pl.when(gx == self.via(s, j))
                    def _():
                        for h in range(PIECES):
                            self.part(s, j, h).wait_send()

        def start_far(self):
            self.start(1, left)
            self.start(-1, right)

        def start_near(self):
            self.start(-1, left)
            self.start(1, right)

        def arrive_near(self):
            self.arrive(1, left)
            self.arrive(-1, right)

        def arrive_far(self):
            self.arrive(-1, left)
            self.arrive(1, right)

    barrier = pltpu.get_barrier_semaphore()
    expect = jnp.int32(0)
    for d in DIRS:
        @pl.when(has[d])
        def _():
            pl.semaphore_signal(barrier, inc=1, device_id=(gx, gy + d[0], gz + d[1]), device_id_type=MESH)
        expect = expect + has[d].astype(jnp.int32)
    for s in (-1, 1):
        @pl.when(has_x[s])
        def _():
            pl.semaphore_signal(barrier, inc=1, device_id=(gx + s, gy, gz), device_id_type=MESH)
        expect = expect + has_x[s].astype(jnp.int32)
    if relay:
        pairs = []
        for s in (-1, 1):
            e = mid if s == 1 else mid + 1
            pairs += [(e, e - s * j) for j in (2, 3)] + [(e - s * j, e + s) for j in (1, 2, 3)]
        for a, b in pairs:
            @pl.when(gx == b)
            def _():
                pl.semaphore_signal(barrier, inc=1, device_id=(jnp.int32(a), gy, gz), device_id_type=MESH)
            expect = expect + (gx == a).astype(jnp.int32)

    loads = [pltpu.make_async_copy(a, b, lsem.at[i]) for i, (a, b) in enumerate(
        ((f_hbm, f), (bz_hbm, bz), (bx_hbm, bx), (by_hbm, by), (ex_hbm, ex), (ey_hbm, ey), (ez_hbm, ez), (rea_hbm, rea)))]
    for c in loads:
        c.start()
    for c in loads[:7]:
        c.wait()

    def edge(x, width):
        ln = lanes(x.shape[0])
        return jnp.where((ln < width) | (ln >= 128 - width), x, 0.0)

    def pack_one(dst, load, g, first, count, stride, masked):
        acc = None
        for i in range(count):
            x = load(first + i)
            if masked:
                x = edge(x, stride // 2)
            if i:
                x = roll(x, stride * i)
            acc = x if acc is None else acc + x
        dst[g] = acc

    def pack(dst, load, slabs, per, stride, masked):
        def body(g, c):
            pack_one(dst, load, g, g * per, per, stride, masked)
            return c
        full = slabs // per
        lax.fori_loop(0, full, body, 0)
        if slabs % per:
            pack_one(dst, load, full, full * per, slabs % per, stride, masked)

    def low_part(rows, stride):
        ln = lanes(rows)
        return (lax.rem(ln, stride) < stride // 2) & (ln < 128 - stride // 2 if stride == 18 else ln >= 0)

    def zero_missing(buf_of):
        for d in DIRS:
            bufs = buf_of(d)
            if bufs:
                @pl.when(jnp.logical_not(has[(-d[0], -d[1])]))
                def _():
                    for b in bufs:
                        b[...] = jnp.zeros(b.shape, F32)

    def halo_items(src, from0, x0, nx, dst, packed, recv, g0, groups):
        rows = {0: (0, 24, 0), 1: (16, 8, 32), -1: (0, 8, 24)}

        def items(d):
            s, n, t = rows[d[0]]
            if d[1] == 0:
                return [(src.at[pl.ds(from0, nx), pl.ds(s, n)], dst.at[pl.ds(x0, nx), pl.ds(t, n)])]
            return [(packed.at[pl.ds(g0, groups), pl.ds(s, n)],
                     recv.at[0 if d[1] == 1 else 1, pl.ds(g0, groups), pl.ds(t, n)])]
        return items

    def fold_items(a0, n, packed, recv_f, recv_c, recv_y):
        rows = {1: 24, -1: 32}

        def items(d):
            z = 0 if d[1] == 1 else 1
            y = 0 if d[0] == 1 else 1
            if d[1] == 0:
                return [(U0.at[pl.ds(a0, n), pl.ds(rows[d[0]], 8)], recv_y.at[y])]
            if d[0] == 0:
                return [(packed.at[:, pl.ds(0, 24)], recv_f.at[z])]
            return [(packed.at[:, pl.ds(rows[d[0]], 8)], recv_c.at[y, z])]
        return items

    def layer_items(v0, n, row_s, row_r, packed, recv_z, recv_c):
        def items(d):
            z = 0 if d[1] == 1 else 1
            y = 0 if d[0] == 1 else 1
            if d[1] == 0:
                s, t = ((16, 40), (0, 24))[y]
                return [(V0.at[pl.ds(v0, n), pl.ds(s, 8)], V0.at[pl.ds(v0, n), pl.ds(t, 8)]),
                        (row_s.at[y], row_r.at[y])]
            if d[0] == 0:
                return [(packed, recv_z.at[z])]
            return [(packed.at[:, pl.ds(8 if y == 0 else 0, 16)], recv_c.at[y, z])]
        return items

    def x_halo(b):
        return {1: b.at[pl.ds(32, 8), pl.ds(0, 24)], -1: b.at[pl.ds(24, 8), pl.ds(0, 24)]}

    def x_edge(b):
        return {1: b.at[pl.ds(16, 8)], -1: b.at[pl.ds(0, 8)]}

    xf = XX(x_edge(f), x_halo(E0), 8, STRAIGHT8, RB8a)
    xr = XX(x_edge(rea), x_halo(RE0), 8, STRAIGHT8, RB8c)
    xn, xfar = pick(32, 24), pick(24, 32)
    fA = YZ(halo_items(f, 0, 0, 24, E0, pfA, rfA, 0, 3))
    fN = YZ(halo_items(E0, xn, xn, 8, E0, pfB, rfB, 0, 1))
    fF = YZ(halo_items(E0, xfar, xfar, 8, E0, pfB, rfB, 1, 1))
    rA = YZ(halo_items(RE0, 0, 0, 40, RE0, pr, rr, 0, 5))
    aF, aN = pick(24, 0), pick(0, 16)
    m1F = YZ(fold_items(aF, 16, pmF, rmfF, rmcF, rmyF))
    m1N = YZ(fold_items(aN, 24, pmN, rmfN, rmcN, rmyN))
    m2 = XX({1: S.at[pl.ds(25, 16)], -1: S.at[pl.ds(1, 16)]},
            {1: X17.at[0, pl.ds(1, 16)], -1: X17.at[1, pl.ds(0, 16)]}, 16, STRAIGHT16, RB16)
    m2b = XX({1: S.at[pl.ds(24, 1)], -1: S.at[pl.ds(17, 1)]},
             {1: X17.at[0, pl.ds(0, 1)], -1: X17.at[1, pl.ds(16, 1)]}, 1)
    vN, vF = pick(0, 17), pick(25, 0)
    m3N = YZ(layer_items(vN, 25, RN, RRN, pvN, rvzN, rvcN))
    m3F = YZ(layer_items(vF, 17, RF, RRF, pvF, rvzF, rvcF))
    eF, eN = pick(32, 0), pick(0, 32)
    l2F = YZ(fold_items(eF, 8, plF, rlfF, rlcF, rlyF))
    l2N = YZ(fold_items(eN, 8, plN, rlfN, rlcN, rlyN))
    l2O = YZ(fold_items(8, 24, plO, rlfO, rlcO, rlyO))
    x2 = XX({1: S.at[pl.ds(33, 8)], -1: S.at[pl.ds(1, 8)]}, {1: X2.at[0], -1: X2.at[1]}, 8, STRAIGHT8, RB8b)

    E0[pl.ds(0, 24), pl.ds(0, 24)] = f[...]
    pack(pfA, lambda i: f[i], 24, 8, 16, True)

    wz32[...] = jnp.zeros((256, 256), F32)
    wz32[0:128, 0:144] = bz[8:136, :]
    wz32[128:136, 0:144] = bz[136:144, :]
    wz32[248:256, 0:144] = bz[0:8, :]
    for w, table, turned in ((wzf, wz32[...], True), (wzb, wz32[...].T, False)):
        hi, lo = split(table)
        w[0:128] = hi[0:128]
        w[128:256] = hi[0:128]
        w[256:384] = lo[0:128]
        hi, lo = hi.astype(F32)[128:256], lo.astype(F32)[128:256]
        if turned:
            tail = jnp.concatenate([hi[0:8], hi[120:128], hi[0:8], lo[120:128], lo[0:8],
                                    jnp.zeros((80, 256), F32), hi[120:128]], axis=0)
        else:
            tail = jnp.concatenate([hi[0:16], hi[0:16], lo[0:16], jnp.zeros((80, 256), F32)], axis=0)
        w[384:512] = tail.astype(BF16)

    def blocks(w, m):
        wxy32[...] = jnp.zeros((80, 256), F32)
        hi, lo = split(m)
        hi, lo = hi.astype(F32), lo.astype(F32)
        for j, part in enumerate((hi, hi, lo)):
            wxy32[0:40, 80 * j:80 * j + 40] = part
            wxy32[40:80, 80 * j + 40:80 * j + 80] = part
        w[...] = wxy32[...].astype(BF16)

    x_nat, y_nat = bx[...], by[...]
    x_circ = jnp.concatenate([x_nat[8:40], x_nat[0:8]], axis=0)
    y_circ = jnp.concatenate([y_nat[8:40], y_nat[0:8]], axis=0)
    blocks(wxf, x_circ.T)
    blocks(wxb, x_nat)
    blocks(wyf, y_circ.T)
    blocks(wyb, y_circ)

    column = lax.broadcasted_iota(jnp.int32, (40, 128), 0)
    exc = lax.fori_loop(0, 40, lambda p, c: jnp.where(column == p, ex[p], c), jnp.zeros((40, 128), F32), unroll=8)
    ez0 = lax.fori_loop(0, 128, lambda p, c: jnp.where(lane == p, ez[p], c), jnp.ones((8, 128), F32), unroll=8)
    ez1 = lax.fori_loop(0, 16, lambda p, c: jnp.where(lane == p, ez[p + 128], c), jnp.ones((8, 128), F32), unroll=8)
    ez0, ez1 = (jnp.concatenate([e] * 5, axis=0) for e in (ez0, ez1))

    first16 = lanes(40) < 16

    def table(g, c):
        acc = None
        for i in range(8):
            base = exc + ey[8 * g + i]
            inv[8 * g + i] = 1.0 / (base + ez0)
            tail = jnp.where(first16, 1.0 / (base + ez1), 0.0)
            acc = tail if acc is None else acc + roll(tail, 16 * i)
        invp[g] = acc
        return c
    lax.fori_loop(0, 5, table, 0)
    invp[5] = jnp.zeros((40, 128), F32)
    TP[5] = jnp.zeros((40, 128), F32)

    loads[7].wait()
    RE0[pl.ds(0, 24), pl.ds(0, 24)] = rea[...]

    def zrows(b, x0, nx, t):
        for i in range(nx // 8):
            b[pl.ds(x0 + 8 * i, 8), pl.ds(t, 8)] = jnp.zeros((8, 8, 128), F32)

    for s, x0 in ((-1, 32), (1, 24)):
        @pl.when(jnp.logical_not(has_x[s]))
        def _():
            for b in (E0, RE0):
                b[pl.ds(x0, 8), pl.ds(0, 24)] = jnp.zeros((8, 24, 128), F32)
            X17[0 if s == -1 else 1] = jnp.zeros((17, 24, 128), F32)
            X2[0 if s == -1 else 1] = jnp.zeros((8, 24, 128), F32)
    for s, t, tv in ((-1, 32, 40), (1, 24, 24)):
        @pl.when(jnp.logical_not(has_y[s]))
        def _():
            for b in (E0, RE0):
                zrows(b, 0, 40, t)
            zrows(V0, 0, 40, tv)
            V0[pl.ds(40, 2), pl.ds(tv, 8)] = jnp.zeros((2, 8, 128), F32)
            for b in (RRN, RRF, rmyF, rmyN, rlyF, rlyN, rlyO):
                b[0 if s == -1 else 1] = jnp.zeros(b.shape[1:], F32)

    def missing(d):
        z = 0 if d[1] == 1 else 1
        y = 0 if d[0] == 1 else 1
        t, n = {0: (0, 24), 1: (32, 8), -1: (24, 8)}[d[0]]
        if d[1] == 0:
            return []
        out_ = [b.at[z, :, pl.ds(t, n)] for b in (rfA, rfB, rr)]
        if d[0] == 0:
            return out_ + [b.at[z] for b in (rmfF, rmfN, rlfF, rlfN, rlfO, rvzN, rvzF)]
        return out_ + [b.at[y, z] for b in (rmcF, rmcN, rlcF, rlcN, rlcO, rvcN, rvcF)]
    zero_missing(missing)
    S[0] = jnp.zeros((24, 128), F32)
    S[41] = jnp.zeros((24, 128), F32)

    pl.semaphore_wait(barrier, expect)

    def unpack_group(recv, g, dst1, x0):
        both = jnp.where(low_part(40, 16), recv[1, g], recv[0, g])
        for i in range(8):
            dst1[x0 + i] = edge(roll(both, -16 * i), 8)

    def unpack_halo(recv, groups, dst1):
        def body(g, c):
            unpack_group(recv, g, dst1, 8 * g)
            return c
        lax.fori_loop(0, groups, body, 0)

    def cat3(x0, x1):
        h0, l0 = split(x0)
        h1 = x1.astype(BF16).astype(F32)
        l1 = x1 - h1
        tail = (h1 + roll(l1, 16) + roll(h1, 32)).astype(BF16)
        return jnp.concatenate([h0, l0, h0, tail], axis=1)

    def stack3(x):
        hi, lo = split(x)
        return jnp.concatenate([hi, lo, hi], axis=0)

    def forward_chunk(c, _):
        x0 = E0[pl.ds(8 * c, 8)].reshape(320, 128)
        x1 = E1[pl.ds(8 * c, 8)].reshape(320, 128)
        z = mm(cat3(x0, x1), wzf[...])
        for i in range(4):
            y = mm(wyf[:, 0:240], stack3(z[80 * i:80 * i + 80]))
            T0[pl.ds(320 * c + 80 * i, 80), :] = y[:, 0:128]
            T1[pl.ds(320 * c + 80 * i, 80), :] = y[:, 128:256]
        return _

    def four(load):
        x = [load(i) for i in range(4)]
        return jnp.concatenate([jnp.concatenate(x[0:2], axis=0), jnp.concatenate(x[2:4], axis=0)], axis=1)

    def divide(x, scale):
        m = mm(wxf[:, 0:240], stack3(x))
        m = mm(wxb[:, 0:240], stack3(m * scale))
        return [m[40 * (i % 2):40 * (i % 2) + 40, 128 * (i // 2):128 * (i // 2) + 128] for i in range(4)]

    def middle():
        def at(q):
            return pl.ds(q, 40, stride=40)

        def group(g, c):
            acc = None
            for i in range(8):
                t = T1[at(8 * g + i), :]
                acc = t if acc is None else acc + roll(t, 16 * i)
            TP[g] = acc
            for h in range(2):
                q = 8 * g + 4 * h
                for i, m in enumerate(divide(four(lambda i: T0[at(q + i), :]), four(lambda i: inv[q + i]))):
                    T0[at(q + i), :] = m
            return c
        lax.fori_loop(0, 5, group, 0, unroll=True)
        tails = divide(four(lambda i: TP[i]), four(lambda i: invp[i]))
        tails += divide(four(lambda i: TP[4 if i == 0 else 5]), four(lambda i: invp[4 if i == 0 else 5]))[0:1]
        for g in range(5):
            for i in range(8):
                T1[at(8 * g + i), :] = jnp.where(first16, roll(tails[g], -16 * i), 0.0)

    def back_chunk(c, _):
        parts = []
        for i in range(4):
            x = jnp.concatenate([T0[pl.ds(320 * c + 80 * i, 80), :], T1[pl.ds(320 * c + 80 * i, 80), :]], axis=1)
            parts.append(mm(wyb[:, 0:240], stack3(x)))
        y = jnp.concatenate(parts, axis=0)
        z = mm(cat3(y[:, 0:128], y[:, 128:256]), wzb[...])
        U0[pl.ds(8 * c, 8)] = z[:, 0:128].reshape(8, 40, 128)
        U1[pl.ds(8 * c, 8)] = z[:, 128:256].reshape(8, 40, 128)
        return _

    def fold(a0, groups, recv_f, recv_c, recv_y):
        def body(g, c):
            both = jnp.where(low_part(24, 16), recv_f[0, g], recv_f[1, g])
            low = low_part(8, 16)
            first = jnp.where(low, recv_c[0, 0, g], recv_c[0, 1, g])
            last = jnp.where(low, recv_c[1, 0, g], recv_c[1, 1, g])
            both = both + jnp.concatenate([first, jnp.zeros((8, 128), F32), last], axis=0)
            for i in range(8):
                t = 8 * g + i
                zpart = edge(roll(both, -16 * i), 8)
                ypart = jnp.concatenate([recv_y[0, t], jnp.zeros((8, 128), F32), recv_y[1, t]], axis=0)
                S[a0 + t + 1] = U0[a0 + t, pl.ds(0, 24)] + (zpart + ypart)
            return c
        lax.fori_loop(0, groups, body, 0)

    def build(v0, side):
        def body(i, c):
            V0[v0 + i, pl.ds(0, 24)] = S[v0 + i] + X17[side, i]
            return c
        lax.fori_loop(0, 17, body, 0)

    def rows_out(rows, v0, n):
        rows[...] = jnp.zeros(rows.shape, F32)
        for i in range(n):
            rows[0, i:i + 1, :] = V0[v0 + i, 15:16, :]
            rows[1, i:i + 1, :] = V0[v0 + i, 8:9, :]

    def rows_in(rows, v0, n):
        for i in range(n):
            V0[v0 + i, 39:40, :] = rows[0, i:i + 1, :]
            V0[v0 + i, 32:33, :] = rows[1, i:i + 1, :]

    def unpack_layer(v0, n, recv_z, recv_c):
        def one(g, count):
            face = jnp.where(low_part(24, 18), recv_z[1, g], recv_z[0, g])
            low = low_part(16, 18)
            lo_y = jnp.where(low, recv_c[0, 1, g], recv_c[0, 0, g])
            hi_y = jnp.where(low, recv_c[1, 1, g], recv_c[1, 0, g])
            between = jnp.where(sub == 0, hi_y[8:16], lo_y[0:8])
            both = jnp.concatenate([face, hi_y[0:8], between, lo_y[8:16]], axis=0)
            for i in range(count):
                V1[v0 + g * 7 + i] = edge(roll(both, -18 * i), 9)

        def body(g, c):
            one(g, 7)
            return c
        lax.fori_loop(0, n // 7, body, 0)
        one(n // 7, n % 7)

    row = lax.broadcasted_iota(jnp.int32, (40, 128), 0)
    ln = lanes(40)
    inside_y = jnp.logical_not(((row >= 24) & (row < 32) & jnp.logical_not(has_y[1]))
                               | ((row >= 32) & jnp.logical_not(has_y[-1])))
    mask0 = jnp.where(inside_y, 1.0, 0.0)
    mask1 = jnp.where(inside_y & (((ln < 8) & has_z[1]) | ((ln >= 120) & has_z[-1])), 1.0, 0.0)
    ln48 = lanes(48)

    def shifts(v0, v1):
        p0, p1 = roll(v0, -1), roll(v1, -1)
        n0, n1 = roll(v0, 1), roll(v1, 1)
        top, bottom = ln48 == 127, ln48 == 0
        z0 = jnp.where(top, p1, p0) + jnp.where(bottom, n1, n0)
        z1 = jnp.where(top, p0, p1) + jnp.where(bottom, n0, n1)
        return z0 + 2.0 * v0, z1 + 2.0 * v1

    def ext(x):
        return jnp.concatenate([x[0:32], x[40:48]], axis=0)

    def level(v, c):
        A0[v], A1[v] = shifts(V0[v], V1[v])
        return c

    def stencil(a, c):
        x = jnp.where(a < 8, a + 32, a - 8)
        inside = jnp.where(((a < 8) & jnp.logical_not(has_x[-1])) | ((a >= 32) & jnp.logical_not(has_x[1])), 0.0, 1.0)
        for V, A, E, RE, m in ((V0, A0, E0, RE0, mask0), (V1, A1, E1, RE1, mask1)):
            v, z = V[a + 1], A[a + 1]
            total = A[a] + A[a + 2] + 2.0 * z
            along = 0.25 * v + 0.0625 * total
            k = 6.0 * v - 0.25 * (V[a] + V[a + 2] + z) - 0.125 * total
            k = k - (pltpu.roll(along, 47, 0) + pltpu.roll(along, 1, 0))
            E[x] = (E[x] - (RE[x] * ext(v) + ext(k))) * (m * inside)
        return c

    xf.start_far()
    xf.start_near()
    fA.start()
    xf.forward()
    fA.arrive()
    unpack_halo(rfA, 3, E1)
    lax.fori_loop(0, 3, forward_chunk, 0, unroll=True)
    for arrive, x0, g, stage in ((xf.arrive_near, xn, 0, fN), (xf.arrive_far, xfar, 1, fF)):
        arrive()
        pack_one(pfB, lambda i: E0[x0 + i, pl.ds(0, 24)], g, 0, 8, 16, True)
        stage.start()
        if g:
            xr.start_far()
            xr.start_near()
        stage.arrive()
        unpack_group(rfB, g, E1, x0)
        forward_chunk(x0 // 8, 0)
    middle()
    bF, bN = pick(3, 0), pick(0, 2)
    lax.fori_loop(0, 2, lambda j, c: back_chunk(bF + j, c), 0, unroll=True)
    pack(pmF, lambda i: U1[aF + i], 16, 8, 16, False)
    m1F.start()
    lax.fori_loop(0, 3, lambda j, c: back_chunk(bN + j, c), 0, unroll=True)
    pack(pmN, lambda i: U1[aN + i], 24, 8, 16, False)
    m1N.start()
    xr.forward()
    m1F.arrive()
    fold(aF, 2, rmfF, rmcF, rmyF)
    m2.start_far()
    m1N.arrive()
    fold(aN, 3, rmfN, rmcN, rmyN)
    m2b.start_far()
    m2.start_near()
    m2b.start_near()
    m2.forward()

    m2.arrive_near()
    m2b.arrive_near()
    build(pick(0, 25), pick(0, 1))
    for i in range(8):
        V0[17 + i, pl.ds(0, 24)] = S[17 + i]
    for s, v in ((-1, 0), (1, 33)):
        @pl.when(jnp.logical_not(has_x[s]))
        def _():
            V0[pl.ds(v, 9), pl.ds(0, 24)] = jnp.zeros((9, 24, 128), F32)
    rows_out(RN, vN, 25)
    pack(pvN, lambda i: V0[vN + i, pl.ds(0, 24)], 25, 7, 18, True)
    m3N.start()
    xr.arrive_near()
    xr.arrive_far()
    pack(pr, lambda i: RE0[i, pl.ds(0, 24)], 40, 8, 16, True)
    rA.start()
    m3N.arrive()
    for stage in (fA, fN, fF, xf, m1F, m1N):
        stage.sent()
    rows_in(RRN, vN, 25)
    unpack_layer(vN, 25, rvzN, rvcN)
    l0 = pick(0, 18)
    lax.fori_loop(0, 24, lambda i, c: level(l0 + i, c), 0, unroll=3)
    rA.arrive()
    unpack_halo(rr, 5, RE1)
    s0 = pick(0, 18)
    lax.fori_loop(0, 22, lambda i, c: stencil(s0 + i, c), 0, unroll=2)
    cN, cF = pick(0, 3), pick(2, 0)
    lax.fori_loop(0, 2, lambda j, c: forward_chunk(lax.rem(cN + j + 4, 5), c), 0, unroll=True)

    m2.arrive_far()
    m2b.arrive_far()
    build(pick(25, 0), pick(1, 0))
    rows_out(RF, vF, 17)
    pack(pvF, lambda i: V0[vF + i, pl.ds(0, 24)], 17, 7, 18, True)
    m3F.start()
    m3F.arrive()
    rows_in(RRF, vF, 17)
    unpack_layer(vF, 17, rvzF, rvcF)
    l1 = pick(24, 0)
    lax.fori_loop(0, 18, lambda i, c: level(l1 + i, c), 0, unroll=3)
    s1 = pick(22, 0)
    lax.fori_loop(0, 18, lambda i, c: stencil(s1 + i, c), 0, unroll=6)

    lax.fori_loop(0, 3, lambda j, c: forward_chunk(lax.rem(cF + j + 4, 5), c), 0, unroll=True)
    middle()
    for a0, packed, stage in ((eF, plF, l2F), (eN, plN, l2N)):
        back_chunk(a0 // 8, 0)
        pack_one(packed, lambda i: U1[a0 + i], 0, 0, 8, 16, False)
        stage.start()
    lax.fori_loop(1, 4, back_chunk, 0, unroll=True)
    m2.sent()
    m2b.sent()
    l2F.arrive()
    fold(eF, 1, rlfF, rlcF, rlyF)
    x2.start_far()
    pack(plO, lambda i: U1[i + 8], 24, 8, 16, False)
    l2O.start()
    l2N.arrive()
    fold(eN, 1, rlfN, rlcN, rlyN)
    x2.start_near()
    x2.forward()
    l2O.arrive()
    fold(8, 3, rlfO, rlcO, rlyO)
    x2.arrive_near()
    x2.arrive_far()

    def finish(i, c):
        out[i] = V0[i + 9, pl.ds(0, 24)] + (S[i + 9] + X2[0, i])
        out[i + 8] = V0[i + 17, pl.ds(0, 24)] + S[i + 17]
        out[i + 16] = V0[i + 25, pl.ds(0, 24)] + (S[i + 25] + X2[1, i])
        return c
    lax.fori_loop(0, 8, finish, 0)
    for stage in (rA, m3N, m3F, l2F, l2N, l2O, xr, x2):
        stage.sent()


def solution(mesh):
    sizes = tuple(mesh.shape[a] for a in ("gx", "gy", "gz"))

    def local(right_side, reaction, basis_x, basis_y, basis_z, eigen_x, eigen_y, eigen_z):
        def vm(*shape, dtype=F32):
            return pltpu.VMEM(shape, dtype)
        scratch = [vm(24, 24, 128), vm(24, 24, 128), vm(40, 40), vm(40, 40), vm(144, 144),
                   pltpu.SMEM((40,), F32), pltpu.SMEM((40,), F32), pltpu.SMEM((144,), F32)]
        scratch += [vm(40, 40, 128), vm(40, 40, 128), vm(40, 40, 128), vm(40, 40, 128),
                   vm(1600, 128), vm(1600, 128), vm(40, 40, 128), vm(40, 40, 128),
                   vm(42, 48, 128), vm(42, 48, 128), vm(40, 40, 128), vm(42, 24, 128),
                   vm(42, 48, 128), vm(42, 48, 128), vm(6, 40, 128), vm(6, 40, 128),
                   vm(256, 256), vm(80, 256), vm(512, 256, dtype=BF16), vm(512, 256, dtype=BF16)]
        scratch += [vm(80, 256, dtype=BF16)] * 4
        scratch += [vm(3, 24, 128), vm(2, 24, 128), vm(5, 24, 128), vm(2, 40, 128), vm(3, 40, 128),
                    vm(4, 24, 128), vm(3, 24, 128), vm(1, 40, 128), vm(1, 40, 128), vm(3, 40, 128)]
        scratch += [vm(2, 3, 40, 128), vm(2, 2, 40, 128), vm(2, 5, 40, 128),
                    vm(2, 2, 24, 128), vm(2, 3, 24, 128), vm(2, 2, 2, 8, 128), vm(2, 2, 3, 8, 128),
                    vm(2, 16, 8, 128), vm(2, 24, 8, 128),
                    vm(2, 4, 24, 128), vm(2, 3, 24, 128), vm(2, 2, 4, 16, 128), vm(2, 2, 3, 16, 128),
                    vm(2, 32, 128), vm(2, 24, 128), vm(2, 32, 128), vm(2, 24, 128)]
        scratch += [vm(2, n, 24, 128) for n in (1, 1, 3)] + [vm(2, 2, n, 8, 128) for n in (1, 1, 3)]
        scratch += [vm(2, n, 8, 128) for n in (8, 8, 24)]
        scratch += [vm(2, 17, 24, 128), vm(2, 8, 24, 128),
                    vm(8 - STRAIGHT8, 8, 128), vm(16 - STRAIGHT16, 8, 128), vm(8 - STRAIGHT8, 8, 128), vm(8 - STRAIGHT8, 8, 128),
                    pltpu.SemaphoreType.DMA((240,)), pltpu.SemaphoreType.DMA((240,)), pltpu.SemaphoreType.DMA((8,))]
        vmem = pl.BlockSpec(memory_space=pltpu.VMEM)
        hbm = pl.BlockSpec(memory_space=pltpu.HBM)

        def body(*refs):
            kernel(sizes, *refs)

        return pl.pallas_call(
            body,
            out_shape=jax.ShapeDtypeStruct((24, 24, 128), F32),
            in_specs=[hbm] * 8,
            out_specs=vmem,
            scratch_shapes=scratch,
            compiler_params=pltpu.CompilerParams(
                collective_id=0, has_side_effects=True, vmem_limit_bytes=40 * 1024 * 1024),
            cost_estimate=pl.CostEstimate(flops=1200000000, bytes_accessed=2000000, transcendentals=0),
        )(*(pltpu.with_memory_space_constraint(a, pltpu.HBM) for a in (
            right_side, reaction, basis_x, basis_y, basis_z, eigen_x, eigen_y, eigen_z)))

    return jax.shard_map(
        local,
        mesh=mesh,
        in_specs=(P("gx", "gy", "gz"), P("gx", "gy", "gz"), P(), P(), P(), P(), P(), P()),
        out_specs=P("gx", "gy", "gz"),
        check_vma=False,
    )
```
